512 devices in a mesh: seq: 128 (over z, y, core), head: 4 (over x).
Axes of the slice: x: 4, y: 8, z: 8, core: 2. Of those that a mesh axis runs over, the one named last changes fastest.
Arguments:
- queries: bfloat16 [65536, 4096], P(('seq', 'head'))
- image_keys: bfloat16 [512, 512, 512], P('seq', None, 'head')
- image_values: bfloat16 [512, 512, 512], P('seq', None, 'head'), may hold values from -6 to 6
- out_grad: bfloat16 [65536, 4096], P(('seq', 'head')), may hold values from -6 to 6
- tile_counts: int32 [512], replicated, may hold values from 1 to 4, as said below
- block_reads: int32 [128, 2], replicated, may hold values from 0 to 511, as said below
Outputs:
- query_grad: bfloat16 [65536, 4096], P(('seq', 'head'))
- key_grad: bfloat16 [512, 512, 512], P('seq', None, 'head')
- value_grad: bfloat16 [512, 512, 512], P('seq', None, 'head')
The draws below stay inside these ranges and needn't reach their ends.
Inputs may be any that keep to these rules, and one draw needn't show every extreme that they name: `block_reads`: image i is owned by index i // 4 of seq. The 2 images read by the blocks of one index d of seq are all different, and each is owned by an index within 2 of d, cyclically (possibly d itself). No owner owns more than 1 of these 2 images, and some owner owns exactly 1 of them. `tile_counts`: some image has 4 tiles.
All inputs are finite; a program needn't handle non-finite values.
Results may differ from the reference program's by a relative error of at most 0.012.
The reference program's roundings to bfloat16 on the way count: a program that leaves them out, or rounds other values in their place, can miss the bound.
Values may be sent and summed in bfloat16 or wider, within the bound.
A program may use at most 64 MiB of HBM per device.

```python
import jax
import jax.numpy as jnp
from jax import lax

HDIM = 128
HQ = 32
KVH = 4
TILE_TOK = 128
MAX_TILES = 4
READS = 2
SPAN = 2
BLK = 512
NBLK_DEV = 1
IMG_DEV = 4
MAXTOK = 512
TOKENS = 65536
NBLK = 128
NIMG = 512


def draw_queries(key, part):
    key = jax.random.fold_in(key, 11)
    values = jnp.clip(jax.random.normal(key, (TOKENS, HQ * HDIM), jnp.float32), -6.0, 6.0)
    return values.astype(jnp.bfloat16)


def draw_image_keys(key, part):
    key = jax.random.fold_in(key, 12)
    values = jnp.clip(jax.random.normal(key, (NIMG, MAXTOK, KVH * HDIM), jnp.float32), -6.0, 6.0)
    return values.astype(jnp.bfloat16)


def draw_tile_counts(key, part):
    key = jax.random.fold_in(key, 13)
    counts = jax.random.randint(key, (NIMG,), 1, MAX_TILES + 1)
    chosen = jax.random.randint(jax.random.fold_in(key, 1), (), 0, NIMG)
    return counts.at[chosen].set(MAX_TILES).astype(jnp.int32)


def offset_order(key_one):
    return jax.random.permutation(key_one, 2 * SPAN + 1)


def draw_block_reads(key, part):
    key = jax.random.fold_in(key, 14)
    seq_count = NIMG // IMG_DEV
    width = 2 * SPAN + 1
    need_count = NBLK_DEV * READS
    orders = jax.vmap(offset_order)(jax.random.split(key, seq_count))
    starting = jax.random.randint(jax.random.fold_in(key, 2), (seq_count, width), 0, IMG_DEV)
    slot_index = jnp.arange(need_count)
    column = slot_index % width
    layer = slot_index // width
    offsets = orders[:, column] - SPAN
    readers = jnp.arange(seq_count)[:, None]
    owners = (readers + offsets) % seq_count
    local_index = (starting[:, column] + layer[None, :]) % IMG_DEV
    image_ids = owners * IMG_DEV + local_index
    return image_ids.reshape(seq_count * NBLK_DEV, READS).astype(jnp.int32)


def shard_levels(rng, shape, cuts, least, top_value):
    factor_of = 1.0
    for axis_at, shards_of in cuts:
        draws = jax.random.uniform(jax.random.fold_in(jax.random.fold_in(rng, 6), axis_at), (shards_of,), jnp.float32, least / len(cuts), top_value / len(cuts))
        factor_of = factor_of * jnp.repeat(jnp.exp(draws), shape[axis_at] // shards_of).reshape((-1,) + (1,) * (len(shape) - 1 - axis_at))
    return factor_of


def bell_draw(own_key, extent, scale, limit, cuts=(), held_as=jnp.bfloat16):
    result = jax.random.normal(own_key, extent, jnp.float32) * scale
    if len(cuts) > 0:
        result = shard_levels(own_key, extent, cuts, -0.22, 0.18) * result
    return jnp.clip(result, min=-limit, max=limit).astype(held_as)


def setup_inputs(seed: int = 0) -> dict:
    splits = jax.random.split(jax.random.key(seed), 7)
    queries = draw_queries(jax.random.fold_in(splits[6], 71), 0)
    image_keys = draw_image_keys(jax.random.fold_in(splits[6], 71), 0)
    image_values = bell_draw(splits[2], (NIMG, MAXTOK, KVH * HDIM), 1.0, 6.0, ((0, 128), (2, 4)))
    out_grad = bell_draw(splits[3], (TOKENS, HQ * HDIM), 1.0, 6.0, ((0, 512),))
    tile_counts = draw_tile_counts(jax.random.fold_in(splits[6], 71), 0)
    block_reads = draw_block_reads(jax.random.fold_in(splits[6], 71), 0)
    return dict(queries=queries, image_keys=image_keys, image_values=image_values, out_grad=out_grad, tile_counts=tile_counts, block_reads=block_reads)


def block_backward(query_rows, grad_rows, key_rows, value_rows, usable):
    scaling = HDIM ** -0.5
    query_wide = query_rows.astype(jnp.float32)
    grad_wide = grad_rows.astype(jnp.float32)
    key_wide = key_rows.astype(jnp.float32)
    value_wide = value_rows.astype(jnp.float32)
    scores = jnp.einsum("tkgd,skd->kgts", query_wide, key_wide) * scaling
    scores = jnp.where(usable[None, None, None, :], scores, -jnp.inf)
    row_max = jnp.max(scores, axis=-1, keepdims=True)
    unnormed = jnp.exp(scores - row_max)
    attention = unnormed / jnp.sum(unnormed, axis=-1, keepdims=True)
    attention_low = lax.optimization_barrier(attention.astype(jnp.bfloat16))
    attention_back = attention_low.astype(jnp.float32)
    context = jnp.einsum("kgts,skd->tkgd", attention_back, value_wide).astype(jnp.bfloat16)
    context = lax.optimization_barrier(context)
    row_dot = jnp.sum(context.astype(jnp.float32) * grad_wide, axis=-1)
    grad_attn = jnp.einsum("tkgd,skd->kgts", grad_wide, value_wide)
    grad_score = (attention * (grad_attn - jnp.transpose(row_dot, (1, 2, 0))[..., None])).astype(jnp.bfloat16)
    grad_score = lax.optimization_barrier(grad_score).astype(jnp.float32)
    grad_query = (jnp.einsum("kgts,skd->tkgd", grad_score, key_wide) * scaling).astype(jnp.bfloat16)
    grad_key = (jnp.einsum("kgts,tkgd->skd", grad_score, query_wide) * scaling).astype(jnp.bfloat16)
    grad_value = jnp.einsum("kgts,tkgd->skd", attention_back, grad_wide).astype(jnp.bfloat16)
    return grad_query, grad_key, grad_value


def reference(queries, image_keys, image_values, out_grad, tile_counts, block_reads):
    group = HQ // KVH
    query_blocks = queries.reshape(NBLK, BLK, KVH, group, HDIM)
    grad_blocks = out_grad.reshape(NBLK, BLK, KVH, group, HDIM)
    positions = jnp.arange(READS * MAXTOK) % MAXTOK

    def one_block(inputs):
        query_rows, grad_rows, image_ids = inputs
        key_rows = image_keys[image_ids].reshape(READS * MAXTOK, KVH, HDIM)
        value_rows = image_values[image_ids].reshape(READS * MAXTOK, KVH, HDIM)
        limits = jnp.repeat(tile_counts[image_ids] * TILE_TOK, MAXTOK)
        usable = positions < limits
        grad_query, grad_key, grad_value = block_backward(query_rows, grad_rows, key_rows, value_rows, usable)
        return (grad_query.reshape(BLK, HQ * HDIM),
                grad_key.reshape(READS, MAXTOK, KVH * HDIM),
                grad_value.reshape(READS, MAXTOK, KVH * HDIM))

    query_parts, key_parts, value_parts = lax.map(one_block, (query_blocks, grad_blocks, block_reads))
    flat_ids = block_reads.reshape(NBLK * READS)
    key_total = jnp.zeros((NIMG, MAXTOK, KVH * HDIM), jnp.float32).at[flat_ids].add(
        key_parts.reshape(NBLK * READS, MAXTOK, KVH * HDIM).astype(jnp.float32))
    value_total = jnp.zeros((NIMG, MAXTOK, KVH * HDIM), jnp.float32).at[flat_ids].add(
        value_parts.reshape(NBLK * READS, MAXTOK, KVH * HDIM).astype(jnp.float32))
    return (query_parts.reshape(TOKENS, HQ * HDIM), key_total.astype(jnp.bfloat16),
            value_total.astype(jnp.bfloat16))
```

```python
import functools

import jax
import jax.numpy as jnp
from jax import lax
from jax.experimental import pallas as pl
from jax.experimental.pallas import tpu as pltpu
from jax.sharding import PartitionSpec as P

HDIM = 128
TILE = 128
READS = 2
SPAN = 2
WIDTH = 2 * SPAN + 1
SCALE = HDIM ** (-0.5)
SCALE2 = SCALE * 1.4426950408889634
UNIT = 256
PAIRS = UNIT // HDIM
F32 = jnp.float32
BF16 = jnp.bfloat16
MESH = pl.DeviceIdType.MESH
NN = (((1,), (0,)), ((), ()))
NT = (((1,), (1,)), ((), ()))
HOPS = (1, 3, 2)


def dot(a, b, dims):
    return lax.dot_general(a, b, dims, preferred_element_type=F32)


def heads_to_rows(x):
    return jnp.concatenate([x[:, h * HDIM : (h + 1) * HDIM] for h in range(PAIRS)], axis=0)


def kernel(
    sizes,
    counts_ref,
    reads_ref,
    q_hbm,
    k_hbm,
    v_hbm,
    g_hbm,
    dq_hbm,
    dk_hbm,
    dv_hbm,
    own_k,
    own_v,
    put_k,
    put_v,
    got_k,
    got_v,
    ret_k,
    ret_v,
    q_all,
    g_all,
    dq_all,
    keys,
    keys_t,
    values,
    s0,
    d0,
    s1,
    d1,
    att,
    dsc,
    row_max,
    sum_k,
    sum_v,
    low_k,
    low_v,
    out_k,
    out_v,
    own_sem,
    q_sem,
    g_sem,
    qs_sem,
    gs_sem,
    kv_send,
    kv_recv,
    back_send,
    back_recv,
    dq_send,
    dq_recv,
    out_sem,
):
    n_seq, n_head, per_owner, slots, head_cols = sizes
    per_head = head_cols // UNIT
    units = n_head * per_head
    n_tiles = READS * slots // TILE
    tiles = slots // TILE
    s = lax.axis_index("seq")
    x = lax.axis_index("head")

    def along_head(k):
        return lax.rem(x + k, n_head)

    def along_seq(o):
        return lax.rem(s + o + n_seq, n_seq)

    load_k = pltpu.make_async_copy(k_hbm, own_k, own_sem.at[0])
    load_v = pltpu.make_async_copy(v_hbm, own_v, own_sem.at[1])
    load_k.start()
    load_v.start()

    def own_load(u):
        cols = pl.ds(pl.multiple_of(x * head_cols + u * UNIT, UNIT), UNIT)
        return (
            pltpu.make_async_copy(q_hbm.at[:, cols], q_all.at[u], q_sem.at[u]),
            pltpu.make_async_copy(g_hbm.at[:, cols], g_all.at[u], g_sem.at[u]),
        )

    for u in range(per_head):
        for c in own_load(u):
            c.start()

    barrier = pltpu.get_barrier_semaphore()
    offsets = [o for o in range(-SPAN, SPAN + 1) if o != 0]
    for k in range(1, n_head):
        pl.semaphore_signal(barrier, inc=1, device_id=(s, along_head(k)), device_id_type=MESH)
    for o in offsets:
        pl.semaphore_signal(barrier, inc=1, device_id=(along_seq(o), x), device_id_type=MESH)
    pl.semaphore_wait(barrier, n_head - 1 + len(offsets))

    picks = []
    for o in range(-SPAN, SPAN + 1):
        reader = along_seq(o)
        first = reads_ref[reader, 0] - s * per_owner
        second = reads_ref[reader, 1] - s * per_owner
        one = (first >= 0) & (first < per_owner)
        two = (second >= 0) & (second < per_owner)
        picks.append(jnp.where(one, first, jnp.where(two, second, 0)))

    def kv_copy(put, got, o, kind):
        g = o + SPAN
        return pltpu.make_async_remote_copy(
            src_ref=put.at[g],
            dst_ref=got.at[g],
            send_sem=kv_send.at[kind, g],
            recv_sem=kv_recv.at[kind, g],
            device_id=(along_seq(o), x),
            device_id_type=MESH,
        )

    load_k.wait()
    for o in offsets:
        put_k[o + SPAN] = own_k[picks[o + SPAN]]
        kv_copy(put_k, got_k, o, 0).start()
    got_k[SPAN] = own_k[picks[SPAN]]
    load_v.wait()
    for o in offsets:
        put_v[o + SPAN] = own_v[picks[o + SPAN]]
        kv_copy(put_v, got_v, o, 1).start()
    got_v[SPAN] = own_v[picks[SPAN]]

    def share_copy(i, k, src, dst, ssem, rsem):
        u = per_head + (n_head - 1) * i + HOPS.index(k)
        to = along_head(k)
        cols = pl.ds(pl.multiple_of(to * head_cols + i * UNIT, UNIT), UNIT)
        return pltpu.make_async_remote_copy(
            src_ref=src.at[:, cols],
            dst_ref=dst.at[u],
            send_sem=ssem.at[u],
            recv_sem=rsem.at[u],
            device_id=(s, to),
            device_id_type=MESH,
        )

    shares = []
    for i in range(per_head):
        for k in HOPS:
            shares.append(share_copy(i, k, q_hbm, q_all, qs_sem, q_sem))
            shares.append(share_copy(i, k, g_hbm, g_all, gs_sem, g_sem))
    for c in shares:
        c.start()

    def await_share(u):
        for buf, ssem, rsem in ((q_all, qs_sem, q_sem), (g_all, gs_sem, g_sem)):
            pltpu.make_async_remote_copy(
                src_ref=buf.at[u],
                dst_ref=buf.at[u],
                send_sem=ssem.at[u],
                recv_sem=rsem.at[u],
                device_id=(s, along_head(1)),
                device_id_type=MESH,
            ).wait_recv()

    images = [reads_ref[s, j] for j in range(READS)]
    groups = [
        jnp.minimum(lax.rem(s - (images[j] // per_owner) + SPAN + n_seq, n_seq), WIDTH - 1)
        for j in range(READS)
    ]
    limits = [counts_ref[images[j]] for j in range(READS)]
    sum_k[...] = jnp.zeros_like(sum_k)
    sum_v[...] = jnp.zeros_like(sum_v)
    for u in range(per_head):
        for c in own_load(u):
            c.wait()
    for o in offsets:
        kv_copy(put_k, got_k, o, 0).wait()
    for j in range(READS):
        keys[j * slots : (j + 1) * slots, :] = got_k[groups[j]]
    keys_t[...] = keys[...].T
    for o in offsets:
        kv_copy(put_v, got_v, o, 1).wait()
    for j in range(READS):
        values[j * slots : (j + 1) * slots, :] = got_v[groups[j]]

    def usable(i):
        return (i % tiles) < limits[i // tiles]

    chunk = 512
    n_chunks = READS * slots // chunk
    chunk_tiles = chunk // TILE
    halves = ((s0, d0), (s1, d1))

    def score_chunk(q, g, half, c):
        s_ref, d_ref = half
        rows = pl.ds(c * chunk, chunk)
        score = dot(keys[rows, :], q, NT)
        s_ref[rows, :] = score
        d_ref[rows, :] = dot(values[rows, :], g, NT)
        return [
            jnp.max(score[t * TILE : (t + 1) * TILE].reshape(TILE // 8, 8, UNIT), axis=0)
            for t in range(chunk_tiles)
        ]

    def finish_max(tops):
        top = None
        for i in range(n_tiles):
            one = jnp.where(usable(i), tops[i], -jnp.inf)
            top = one if top is None else jnp.maximum(top, one)
        return jnp.max(top, axis=0, keepdims=True) * SCALE2

    def first_scores():
        q, g = heads_to_rows(q_all[0]), heads_to_rows(g_all[0])
        tops = []
        for c in range(n_chunks):
            tops += score_chunk(q, g, halves[0], c)
        row_max[0:1, :] = finish_max(tops)

    def step(u, b, more):
        s_ref, d_ref = halves[b]
        top = row_max[b : b + 1, :]
        total = jnp.zeros((8, UNIT), F32)
        weighted = jnp.zeros((8, UNIT), F32)
        tops = []
        if more:
            qn, gn = heads_to_rows(q_all[u + 1]), heads_to_rows(g_all[u + 1])
        for c in range(n_chunks):
            if more:
                tops += score_chunk(qn, gn, halves[1 - b], c)
            for t in range(chunk_tiles):
                i = c * chunk_tiles + t
                rows = pl.ds(i * TILE, TILE)
                shift = jnp.where(usable(i), top, jnp.inf)
                p = jnp.exp2(s_ref[rows, :] * SCALE2 - shift)
                s_ref[rows, :] = p
                total = total + jnp.sum(p.reshape(TILE // 8, 8, UNIT), axis=0)
                weighted = weighted + jnp.sum(
                    (p * d_ref[rows, :]).reshape(TILE // 8, 8, UNIT), axis=0
                )
        if more:
            row_max[1 - b : 2 - b, :] = finish_max(tops)
        inverse = 1.0 / jnp.sum(total, axis=0, keepdims=True)
        row_dot = jnp.sum(weighted, axis=0, keepdims=True) * inverse
        q, g = heads_to_rows(q_all[u]), heads_to_rows(g_all[u])
        dq = None
        for c in range(n_chunks):
            for t in range(chunk_tiles):
                rows = pl.ds((c * chunk_tiles + t) * TILE, TILE)
                a = s_ref[rows, :] * inverse
                att[rows, :] = a.astype(BF16)
                dsc[rows, :] = (a * (d_ref[rows, :] - row_dot)).astype(BF16)
            rows = pl.ds(c * chunk, chunk)
            sum_v[rows, :] += dot(att[rows, :], g, NN)
            sum_k[rows, :] += dot(dsc[rows, :], q, NN)
            part = dot(keys_t[:, c * chunk : (c + 1) * chunk], dsc[rows, :], NN)
            dq = part if dq is None else dq + part
        dq = (dq * SCALE).T.astype(BF16)
        for h in range(PAIRS):
            dq_all[u, :, h * HDIM : (h + 1) * HDIM] = dq[h * HDIM : (h + 1) * HDIM]

    def dq_own(u):
        cols = pl.ds(pl.multiple_of(x * head_cols + u * UNIT, UNIT), UNIT)
        return pltpu.make_async_copy(dq_all.at[u], dq_hbm.at[:, cols], dq_send.at[u])

    def dq_copy(u):
        r = u - per_head
        i = lax.div(r, n_head - 1)
        h = lax.rem(r, n_head - 1)
        hop = jnp.where(h == 0, HOPS[0], jnp.where(h == 1, HOPS[1], HOPS[2]))
        cols = pl.ds(pl.multiple_of(x * head_cols + i * UNIT, UNIT), UNIT)
        return pltpu.make_async_remote_copy(
            src_ref=dq_all.at[u],
            dst_ref=dq_hbm.at[:, cols],
            send_sem=dq_send.at[u],
            recv_sem=dq_recv.at[u],
            device_id=(s, lax.rem(x - hop + n_head, n_head)),
            device_id_type=MESH,
        )

    first_scores()
    for u in range(per_head - 1):
        step(u, u % 2, True)
        dq_own(u).start()
    await_share(per_head)
    step(per_head - 1, (per_head - 1) % 2, True)
    dq_own(per_head - 1).start()

    def two(j, carry):
        u = per_head + 2 * j
        await_share(u + 1)
        step(u, 0, True)
        dq_copy(u).start()
        await_share(u + 2)
        step(u + 1, 1, True)
        dq_copy(u + 1).start()
        return carry

    lax.fori_loop(0, (units - per_head) // 2 - 1, two, 0)
    await_share(units - 1)
    step(units - 2, 0, True)
    dq_copy(units - 2).start()
    step(units - 1, 1, False)
    dq_copy(units - 1).start()

    def back_copy(put, got, o, kind):
        g = o + SPAN
        return pltpu.make_async_remote_copy(
            src_ref=put.at[g],
            dst_ref=got.at[g],
            send_sem=back_send.at[kind, g],
            recv_sem=back_recv.at[kind, g],
            device_id=(along_seq(-o), x),
            device_id_type=MESH,
        )

    which = []
    for g in range(WIDTH):
        which.append(jnp.where(groups[0] == g, 0, jnp.where(groups[1] == g, 1, READS)))
    for low, total, factor, put, got, kind in (
        (low_v, sum_v, None, put_v, ret_v, 1),
        (low_k, sum_k, SCALE, put_k, ret_k, 0),
    ):
        for j in range(READS):
            block = total[j * slots : (j + 1) * slots, :]
            low[j] = (block if factor is None else block * factor).astype(BF16)
        low[READS] = jnp.zeros(low.shape[1:], BF16)
        for o in offsets:
            put[o + SPAN] = low[which[o + SPAN]]
            back_copy(put, got, o, kind).start()
        got[SPAN] = low[which[SPAN]]

    for put, got, kind, out, hbm in (
        (put_v, ret_v, 1, out_v, dv_hbm),
        (put_k, ret_k, 0, out_k, dk_hbm),
    ):
        for o in offsets:
            back_copy(put, got, o, kind).wait()
        for i in range(per_owner):
            acc = jnp.zeros(out.shape[1:], F32)
            for g in range(WIDTH):
                acc = acc + jnp.where(picks[g] == i, got[g].astype(F32), 0.0)
            out[i] = acc.astype(BF16)
        pltpu.make_async_copy(out, hbm, out_sem.at[kind]).start()

    for c in shares:
        c.wait_send()
    for u in range(per_head):
        dq_own(u).wait()

    def finish(j, carry):
        dq_copy(per_head + j).wait()
        return carry

    lax.fori_loop(0, units - per_head, finish, 0)
    pltpu.make_async_copy(out_v, dv_hbm, out_sem.at[1]).wait()
    pltpu.make_async_copy(out_k, dk_hbm, out_sem.at[0]).wait()


def per_device(queries, image_keys, image_values, out_grad, tile_counts, block_reads):
    n_seq, n_head = lax.axis_size("seq"), lax.axis_size("head")
    rows, cols = queries.shape
    per_owner, slots, _ = image_keys.shape
    head_cols = cols // n_head
    units = cols // UNIT
    sizes = (n_seq, n_head, per_owner, slots, head_cols)
    smem = pl.BlockSpec(memory_space=pltpu.SMEM)
    anywhere = pl.BlockSpec(memory_space=pl.ANY)
    image = (slots, HDIM)
    span = READS * slots
    vmem = pltpu.VMEM
    dma = pltpu.SemaphoreType.DMA
    query_grad, key_grad, value_grad = pl.pallas_call(
        functools.partial(kernel, sizes),
        out_shape=(
            jax.ShapeDtypeStruct(queries.shape, BF16),
            jax.ShapeDtypeStruct(image_keys.shape, BF16),
            jax.ShapeDtypeStruct(image_values.shape, BF16),
        ),
        in_specs=[smem, smem, anywhere, anywhere, anywhere, anywhere],
        out_specs=[anywhere] * 3,
        scratch_shapes=[
            vmem((per_owner, *image), BF16),
            vmem((per_owner, *image), BF16),
            vmem((WIDTH, *image), BF16),
            vmem((WIDTH, *image), BF16),
            vmem((WIDTH, *image), BF16),
            vmem((WIDTH, *image), BF16),
            vmem((WIDTH, *image), BF16),
            vmem((WIDTH, *image), BF16),
            vmem((units, rows, UNIT), BF16),
            vmem((units, rows, UNIT), BF16),
            vmem((units, rows, UNIT), BF16),
            vmem((span, HDIM), BF16),
            vmem((HDIM, span), BF16),
            vmem((span, HDIM), BF16),
            vmem((span, UNIT), F32),
            vmem((span, UNIT), F32),
            vmem((span, UNIT), F32),
            vmem((span, UNIT), F32),
            vmem((span, UNIT), BF16),
            vmem((span, UNIT), BF16),
            vmem((8, UNIT), F32),
            vmem((span, HDIM), F32),
            vmem((span, HDIM), F32),
            vmem((READS + 1, *image), BF16),
            vmem((READS + 1, *image), BF16),
            vmem((per_owner, *image), BF16),
            vmem((per_owner, *image), BF16),
            dma((2,)),
            dma((units,)),
            dma((units,)),
            dma((units,)),
            dma((units,)),
            dma((2, WIDTH)),
            dma((2, WIDTH)),
            dma((2, WIDTH)),
            dma((2, WIDTH)),
            dma((units,)),
            dma((units,)),
            dma((2,)),
        ],
        compiler_params=pltpu.CompilerParams(
            collective_id=0, has_side_effects=True, vmem_limit_bytes=48 * 1024 * 1024
        ),
        name="cross_attention_backward",
    )(tile_counts, block_reads, queries, image_keys, image_values, out_grad)
    return query_grad, key_grad, value_grad


def solution(mesh):
    in_specs = (
        P(("seq", "head"), None),
        P("seq", None, "head"),
        P("seq", None, "head"),
        P(("seq", "head"), None),
        P(),
        P(),
    )
    out_specs = (P(("seq", "head"), None), P("seq", None, "head"), P("seq", None, "head"))
    return jax.shard_map(
        per_device, mesh=mesh, in_specs=in_specs, out_specs=out_specs, check_vma=False
    )
```

```python
import functools

import jax
import jax.numpy as jnp
from jax import lax
from jax.experimental import pallas as pl
from jax.experimental.pallas import tpu as pltpu
from jax.sharding import PartitionSpec as P

HDIM = 128
TILE = 128
READS = 2
SPAN = 2
WIDTH = 2 * SPAN + 1
SCALE = HDIM ** (-0.5)
SCALE2 = SCALE * 1.4426950408889634
UNIT = 256
PAIRS = UNIT // HDIM
VMEM_LIMIT = 58 * 1024 * 1024
F32 = jnp.float32
BF16 = jnp.bfloat16
MESH = pl.DeviceIdType.MESH
NN = (((1,), (0,)), ((), ()))
NT = (((1,), (1,)), ((), ()))
HOPS = (1, 3, 2)


def dot(a, b, dims):
    return lax.dot_general(a, b, dims, preferred_element_type=F32)


def heads_to_rows(x):
    return jnp.concatenate([x[:, h * HDIM : (h + 1) * HDIM] for h in range(PAIRS)], axis=0)


def kernel(
    sizes,
    counts_hbm,
    reads_hbm,
    q_hbm,
    k_hbm,
    v_hbm,
    g_hbm,
    dq_hbm,
    out_k,
    out_v,
    counts_ref,
    reads_ref,
    own_k,
    own_v,
    put_k,
    put_v,
    got_k,
    got_v,
    ret_k,
    ret_v,
    q_all,
    g_all,
    dq_all,
    keys,
    keys_t,
    values,
    s0,
    d0,
    s1,
    d1,
    att,
    dsc,
    row_max,
    sum_k,
    sum_v,
    low_k,
    low_v,
    own_sem,
    q_sem,
    g_sem,
    qs_sem,
    gs_sem,
    kv_send,
    kv_recv,
    back_send,
    back_recv,
    dq_send,
    dq_recv,
):
    n_seq, n_head, per_owner, slots, head_cols = sizes
    per_head = head_cols // UNIT
    units = n_head * per_head
    n_tiles = READS * slots // TILE
    tiles = slots // TILE
    s = lax.axis_index("seq")
    x = lax.axis_index("head")

    def along_head(k):
        return lax.rem(x + k, n_head)

    def along_seq(o):
        return lax.rem(s + o + n_seq, n_seq)

    load_reads = pltpu.make_async_copy(reads_hbm, reads_ref, own_sem.at[2])
    load_counts = pltpu.make_async_copy(counts_hbm, counts_ref, own_sem.at[3])
    load_reads.start()
    load_counts.start()
    load_k = pltpu.make_async_copy(k_hbm, own_k, own_sem.at[0])
    load_v = pltpu.make_async_copy(v_hbm, own_v, own_sem.at[1])
    load_k.start()
    load_v.start()

    def own_load(u):
        cols = pl.ds(pl.multiple_of(x * head_cols + u * UNIT, UNIT), UNIT)
        return (
            pltpu.make_async_copy(q_hbm.at[:, cols], q_all.at[u], q_sem.at[u]),
            pltpu.make_async_copy(g_hbm.at[:, cols], g_all.at[u], g_sem.at[u]),
        )

    for u in range(per_head):
        for c in own_load(u):
            c.start()

    barrier = pltpu.get_barrier_semaphore()
    offsets = [o for o in range(-SPAN, SPAN + 1) if o != 0]
    for k in range(1, n_head):
        pl.semaphore_signal(barrier, inc=1, device_id=(s, along_head(k)), device_id_type=MESH)
    for o in offsets:
        pl.semaphore_signal(barrier, inc=1, device_id=(along_seq(o), x), device_id_type=MESH)
    pl.semaphore_wait(barrier, n_head - 1 + len(offsets))

    load_reads.wait()
    load_counts.wait()

    picks = []
    for o in range(-SPAN, SPAN + 1):
        reader = along_seq(o)
        first = reads_ref[0, reader] - s * per_owner
        second = reads_ref[1, reader] - s * per_owner
        one = (first >= 0) & (first < per_owner)
        two = (second >= 0) & (second < per_owner)
        picks.append(jnp.where(one, first, jnp.where(two, second, 0)))

    def kv_copy(put, got, o, kind):
        g = o + SPAN
        return pltpu.make_async_remote_copy(
            src_ref=put.at[g],
            dst_ref=got.at[g],
            send_sem=kv_send.at[kind, g],
            recv_sem=kv_recv.at[kind, g],
            device_id=(along_seq(o), x),
            device_id_type=MESH,
        )

    load_k.wait()
    for o in offsets:
        put_k[o + SPAN] = own_k[picks[o + SPAN]]
        kv_copy(put_k, got_k, o, 0).start()
    got_k[SPAN] = own_k[picks[SPAN]]
    load_v.wait()
    for o in offsets:
        put_v[o + SPAN] = own_v[picks[o + SPAN]]
        kv_copy(put_v, got_v, o, 1).start()
    got_v[SPAN] = own_v[picks[SPAN]]

    def share_copy(i, k, src, dst, ssem, rsem):
        u = per_head + (n_head - 1) * i + HOPS.index(k)
        to = along_head(k)
        cols = pl.ds(pl.multiple_of(to * head_cols + i * UNIT, UNIT), UNIT)
        return pltpu.make_async_remote_copy(
            src_ref=src.at[:, cols],
            dst_ref=dst.at[u],
            send_sem=ssem.at[u],
            recv_sem=rsem.at[u],
            device_id=(s, to),
            device_id_type=MESH,
        )

    shares = []
    for i in range(per_head):
        for k in HOPS:
            shares.append(share_copy(i, k, q_hbm, q_all, qs_sem, q_sem))
            shares.append(share_copy(i, k, g_hbm, g_all, gs_sem, g_sem))
    for c in shares:
        c.start()

    def await_share(u):
        for buf, ssem, rsem in ((q_all, qs_sem, q_sem), (g_all, gs_sem, g_sem)):
            pltpu.make_async_remote_copy(
                src_ref=buf.at[u],
                dst_ref=buf.at[u],
                send_sem=ssem.at[u],
                recv_sem=rsem.at[u],
                device_id=(s, along_head(1)),
                device_id_type=MESH,
            ).wait_recv()

    images = [reads_ref[j, s] for j in range(READS)]
    groups = [
        jnp.minimum(lax.rem(s - (images[j] // per_owner) + SPAN + n_seq, n_seq), WIDTH - 1)
        for j in range(READS)
    ]
    limits = [counts_ref[images[j]] for j in range(READS)]
    sum_k[...] = jnp.zeros_like(sum_k)
    sum_v[...] = jnp.zeros_like(sum_v)
    for u in range(per_head):
        for c in own_load(u):
            c.wait()
    for o in offsets:
        kv_copy(put_k, got_k, o, 0).wait()
    for j in range(READS):
        keys[j * slots : (j + 1) * slots, :] = got_k[groups[j]]
    keys_t[...] = keys[...].T
    for o in offsets:
        kv_copy(put_v, got_v, o, 1).wait()
    for j in range(READS):
        values[j * slots : (j + 1) * slots, :] = got_v[groups[j]]

    def usable(i):
        return (i % tiles) < limits[i // tiles]

    chunk = 512
    n_chunks = READS * slots // chunk
    chunk_tiles = chunk // TILE
    halves = ((s0, d0), (s1, d1))

    def score_chunk(q, g, half, c):
        s_ref, d_ref = half
        rows = pl.ds(c * chunk, chunk)
        score = dot(keys[rows, :], q, NT)
        s_ref[rows, :] = score
        d_ref[rows, :] = dot(values[rows, :], g, NT)
        return [
            jnp.max(score[t * TILE : (t + 1) * TILE].reshape(TILE // 8, 8, UNIT), axis=0)
            for t in range(chunk_tiles)
        ]

    def finish_max(tops):
        top = None
        for i in range(n_tiles):
            one = jnp.where(usable(i), tops[i], -jnp.inf)
            top = one if top is None else jnp.maximum(top, one)
        return jnp.max(top, axis=0, keepdims=True) * SCALE2

    def first_scores():
        q, g = heads_to_rows(q_all[0]), heads_to_rows(g_all[0])
        tops = []
        for c in range(n_chunks):
            tops += score_chunk(q, g, halves[0], c)
        row_max[0:1, :] = finish_max(tops)

    def step(u, b, more):
        s_ref, d_ref = halves[b]
        top = row_max[b : b + 1, :]
        total = jnp.zeros((8, UNIT), F32)
        weighted = jnp.zeros((8, UNIT), F32)
        tops = []
        if more:
            qn, gn = heads_to_rows(q_all[u + 1]), heads_to_rows(g_all[u + 1])
        for c in range(n_chunks):
            if more:
                tops += score_chunk(qn, gn, halves[1 - b], c)
            for t in range(chunk_tiles):
                i = c * chunk_tiles + t
                rows = pl.ds(i * TILE, TILE)
                shift = jnp.where(usable(i), top, jnp.inf)
                p = jnp.exp2(s_ref[rows, :] * SCALE2 - shift)
                s_ref[rows, :] = p
                total = total + jnp.sum(p.reshape(TILE // 8, 8, UNIT), axis=0)
                weighted = weighted + jnp.sum(
                    (p * d_ref[rows, :]).reshape(TILE // 8, 8, UNIT), axis=0
                )
        if more:
            row_max[1 - b : 2 - b, :] = finish_max(tops)
        inverse = 1.0 / jnp.sum(total, axis=0, keepdims=True)
        row_dot = jnp.sum(weighted, axis=0, keepdims=True) * inverse
        q, g = heads_to_rows(q_all[u]), heads_to_rows(g_all[u])
        dq = None
        for c in range(n_chunks):
            for t in range(chunk_tiles):
                rows = pl.ds((c * chunk_tiles + t) * TILE, TILE)
                a = s_ref[rows, :] * inverse
                att[rows, :] = a.astype(BF16)
                dsc[rows, :] = (a * (d_ref[rows, :] - row_dot)).astype(BF16)
            rows = pl.ds(c * chunk, chunk)
            sum_v[rows, :] += dot(att[rows, :], g, NN)
            sum_k[rows, :] += dot(dsc[rows, :], q, NN)
            part = dot(keys_t[:, c * chunk : (c + 1) * chunk], dsc[rows, :], NN)
            dq = part if dq is None else dq + part
        dq = (dq * SCALE).T.astype(BF16)
        for h in range(PAIRS):
            dq_all[u, :, h * HDIM : (h + 1) * HDIM] = dq[h * HDIM : (h + 1) * HDIM]

    def dq_own(u):
        cols = pl.ds(pl.multiple_of(x * head_cols + u * UNIT, UNIT), UNIT)
        return pltpu.make_async_copy(dq_all.at[u], dq_hbm.at[:, cols], dq_send.at[u])

    def dq_copy(u):
        r = u - per_head
        i = lax.div(r, n_head - 1)
        h = lax.rem(r, n_head - 1)
        hop = jnp.where(h == 0, HOPS[0], jnp.where(h == 1, HOPS[1], HOPS[2]))
        cols = pl.ds(pl.multiple_of(x * head_cols + i * UNIT, UNIT), UNIT)
        return pltpu.make_async_remote_copy(
            src_ref=dq_all.at[u],
            dst_ref=dq_hbm.at[:, cols],
            send_sem=dq_send.at[u],
            recv_sem=dq_recv.at[u],
            device_id=(s, lax.rem(x - hop + n_head, n_head)),
            device_id_type=MESH,
        )

    first_scores()
    for u in range(per_head - 1):
        step(u, u % 2, True)
        dq_own(u).start()
    await_share(per_head)
    step(per_head - 1, (per_head - 1) % 2, True)
    dq_own(per_head - 1).start()

    def two(j, carry):
        u = per_head + 2 * j
        await_share(u + 1)
        step(u, 0, True)
        dq_copy(u).start()
        await_share(u + 2)
        step(u + 1, 1, True)
        dq_copy(u + 1).start()
        return carry

    lax.fori_loop(0, (units - per_head) // 2 - 1, two, 0)
    await_share(units - 1)
    step(units - 2, 0, True)
    dq_copy(units - 2).start()
    step(units - 1, 1, False)
    dq_copy(units - 1).start()

    def back_copy(put, got, o, kind):
        g = o + SPAN
        return pltpu.make_async_remote_copy(
            src_ref=put.at[g],
            dst_ref=got.at[g],
            send_sem=back_send.at[kind, g],
            recv_sem=back_recv.at[kind, g],
            device_id=(along_seq(-o), x),
            device_id_type=MESH,
        )

    which = []
    for g in range(WIDTH):
        which.append(jnp.where(groups[0] == g, 0, jnp.where(groups[1] == g, 1, READS)))
    for low, total, factor, put, got, kind in (
        (low_v, sum_v, None, put_v, ret_v, 1),
        (low_k, sum_k, SCALE, put_k, ret_k, 0),
    ):
        for j in range(READS):
            block = total[j * slots : (j + 1) * slots, :]
            low[j] = (block if factor is None else block * factor).astype(BF16)
        low[READS] = jnp.zeros(low.shape[1:], BF16)
        for o in offsets:
            put[o + SPAN] = low[which[o + SPAN]]
            back_copy(put, got, o, kind).start()
        got[SPAN] = low[which[SPAN]]

    for put, got, kind, out in (
        (put_v, ret_v, 1, out_v),
        (put_k, ret_k, 0, out_k),
    ):
        for o in offsets:
            back_copy(put, got, o, kind).wait()
        for i in range(per_owner):
            acc = jnp.zeros(out.shape[1:], F32)
            for g in range(WIDTH):
                acc = acc + jnp.where(picks[g] == i, got[g].astype(F32), 0.0)
            out[i] = acc.astype(BF16)

    for c in shares:
        c.wait_send()
    for u in range(per_head):
        dq_own(u).wait()

    def finish(j, carry):
        dq_copy(per_head + j).wait()
        return carry

    lax.fori_loop(0, units - per_head, finish, 0)


def write_out(*refs):
    sem = refs[-1]
    half = (len(refs) - 1) // 2
    copies = [
        pltpu.make_async_copy(refs[i], refs[half + i], sem.at[i]) for i in range(half)
    ]
    for c in copies:
        c.start()
    for c in copies:
        c.wait()


def per_device(queries, image_keys, image_values, out_grad, tile_counts, block_reads):
    n_seq, n_head = lax.axis_size("seq"), lax.axis_size("head")
    rows, cols = queries.shape
    per_owner, slots, _ = image_keys.shape
    head_cols = cols // n_head
    units = cols // UNIT
    sizes = (n_seq, n_head, per_owner, slots, head_cols)
    inside = pl.BlockSpec(memory_space=pltpu.VMEM)
    anywhere = pl.BlockSpec(memory_space=pl.ANY)
    image = (slots, HDIM)
    span = READS * slots
    vmem = pltpu.VMEM
    dma = pltpu.SemaphoreType.DMA
    operands = (tile_counts, block_reads.T, queries, image_keys, image_values, out_grad)
    grads = pl.pallas_call(
        functools.partial(kernel, sizes),
        out_shape=(
            pltpu.VMEM(queries.shape, BF16),
            pltpu.VMEM(image_keys.shape, BF16),
            pltpu.VMEM(image_values.shape, BF16),
        ),
        in_specs=[anywhere, anywhere, anywhere, anywhere, anywhere, anywhere],
        out_specs=[inside] * 3,
        scratch_shapes=[
            pltpu.SMEM(tile_counts.shape, jnp.int32),
            pltpu.SMEM(block_reads.shape[::-1], jnp.int32),
            vmem((per_owner, *image), BF16),
            vmem((per_owner, *image), BF16),
            vmem((WIDTH, *image), BF16),
            vmem((WIDTH, *image), BF16),
            vmem((WIDTH, *image), BF16),
            vmem((WIDTH, *image), BF16),
            vmem((WIDTH, *image), BF16),
            vmem((WIDTH, *image), BF16),
            vmem((units, rows, UNIT), BF16),
            vmem((units, rows, UNIT), BF16),
            vmem((units, rows, UNIT), BF16),
            vmem((span, HDIM), BF16),
            vmem((HDIM, span), BF16),
            vmem((span, HDIM), BF16),
            vmem((span, UNIT), F32),
            vmem((span, UNIT), F32),
            vmem((span, UNIT), F32),
            vmem((span, UNIT), F32),
            vmem((span, UNIT), BF16),
            vmem((span, UNIT), BF16),
            vmem((8, UNIT), F32),
            vmem((span, HDIM), F32),
            vmem((span, HDIM), F32),
            vmem((READS + 1, *image), BF16),
            vmem((READS + 1, *image), BF16),
            dma((4,)),
            dma((units,)),
            dma((units,)),
            dma((units,)),
            dma((units,)),
            dma((2, WIDTH)),
            dma((2, WIDTH)),
            dma((2, WIDTH)),
            dma((2, WIDTH)),
            dma((units,)),
            dma((units,)),
        ],
        compiler_params=pltpu.CompilerParams(
            collective_id=0, has_side_effects=True, vmem_limit_bytes=VMEM_LIMIT
        ),
        name="cross_attention_backward",
    )(*(pltpu.with_memory_space_constraint(a, pltpu.HBM) for a in operands))
    return pl.pallas_call(
        write_out,
        out_shape=[jax.ShapeDtypeStruct(a.shape, a.dtype) for a in grads],
        in_specs=[inside] * 3,
        out_specs=[anywhere] * 3,
        scratch_shapes=[dma((3,))],
        name="write_out",
    )(*(pltpu.with_memory_space_constraint(a, pltpu.VMEM) for a in grads))


def solution(mesh):
    in_specs = (
        P(("seq", "head"), None),
        P("seq", None, "head"),
        P("seq", None, "head"),
        P(("seq", "head"), None),
        P(),
        P(),
    )
    out_specs = (P(("seq", "head"), None), P("seq", None, "head"), P("seq", None, "head"))
    return jax.shard_map(
        per_device, mesh=mesh, in_specs=in_specs, out_specs=out_specs, check_vma=False
    )
```

```python
import functools

import jax
import jax.numpy as jnp
from jax import lax
from jax.experimental import pallas as pl
from jax.experimental.pallas import tpu as pltpu
from jax.sharding import PartitionSpec as P

HDIM = 128
TILE = 128
READS = 2
SPAN = 2
WIDTH = 2 * SPAN + 1
SCALE = HDIM ** (-0.5)
SCALE2 = SCALE * 1.4426950408889634
UNIT = 256
PAIRS = UNIT // HDIM
VMEM_LIMIT = 58 * 1024 * 1024
F32 = jnp.float32
BF16 = jnp.bfloat16
MESH = pl.DeviceIdType.MESH
NN = (((1,), (0,)), ((), ()))
NT = (((1,), (1,)), ((), ()))
HOPS = (1, 3, 2)


def dot(a, b, dims):
    return lax.dot_general(a, b, dims, preferred_element_type=F32)


def heads_to_rows(x):
    return jnp.concatenate([x[:, h * HDIM : (h + 1) * HDIM] for h in range(PAIRS)], axis=0)


def kernel(
    sizes,
    counts_hbm,
    reads_hbm,
    q_hbm,
    k_hbm,
    v_hbm,
    g_hbm,
    dq_hbm,
    out_k,
    out_v,
    counts_ref,
    reads_ref,
    own_k,
    own_v,
    put_k,
    put_v,
    got_k,
    got_v,
    ret_k,
    ret_v,
    q_all,
    g_all,
    dq_all,
    keys,
    keys_t,
    values,
    s0,
    d0,
    s1,
    d1,
    att,
    dsc,
    att_late,
    dsc_late,
    q_rows,
    g_rows,
    row_max,
    sum_k,
    sum_v,
    low_k,
    low_v,
    own_sem,
    q_sem,
    g_sem,
    qs_sem,
    gs_sem,
    kv_send,
    kv_recv,
    back_send,
    back_recv,
    dq_send,
    dq_recv,
):
    n_seq, n_head, per_owner, slots, head_cols = sizes
    per_head = head_cols // UNIT
    units = n_head * per_head
    n_tiles = READS * slots // TILE
    tiles = slots // TILE
    s = lax.axis_index("seq")
    x = lax.axis_index("head")

    def along_head(k):
        return lax.rem(x + k, n_head)

    def along_seq(o):
        return lax.rem(s + o + n_seq, n_seq)

    load_reads = pltpu.make_async_copy(reads_hbm, reads_ref, own_sem.at[2])
    load_counts = pltpu.make_async_copy(counts_hbm, counts_ref, own_sem.at[3])
    load_reads.start()
    load_counts.start()
    load_k = pltpu.make_async_copy(k_hbm, own_k, own_sem.at[0])
    load_v = pltpu.make_async_copy(v_hbm, own_v, own_sem.at[1])
    load_k.start()
    load_v.start()

    def own_load(u):
        cols = pl.ds(pl.multiple_of(x * head_cols + u * UNIT, UNIT), UNIT)
        return (
            pltpu.make_async_copy(q_hbm.at[:, cols], q_all.at[u], q_sem.at[u]),
            pltpu.make_async_copy(g_hbm.at[:, cols], g_all.at[u], g_sem.at[u]),
        )

    for u in range(per_head):
        for c in own_load(u):
            c.start()

    barrier = pltpu.get_barrier_semaphore()
    offsets = [o for o in range(-SPAN, SPAN + 1) if o != 0]
    for k in range(1, n_head):
        pl.semaphore_signal(barrier, inc=1, device_id=(s, along_head(k)), device_id_type=MESH)
    for o in offsets:
        pl.semaphore_signal(barrier, inc=1, device_id=(along_seq(o), x), device_id_type=MESH)
    pl.semaphore_wait(barrier, n_head - 1 + len(offsets))

    def share_copy(i, k, src, dst, ssem, rsem):
        u = per_head + (n_head - 1) * i + HOPS.index(k)
        to = along_head(k)
        cols = pl.ds(pl.multiple_of(to * head_cols + i * UNIT, UNIT), UNIT)
        return pltpu.make_async_remote_copy(
            src_ref=src.at[:, cols],
            dst_ref=dst.at[u],
            send_sem=ssem.at[u],
            recv_sem=rsem.at[u],
            device_id=(s, to),
            device_id_type=MESH,
        )

    shares = []
    for i in range(per_head):
        for k in HOPS:
            shares.append(share_copy(i, k, q_hbm, q_all, qs_sem, q_sem))
            shares.append(share_copy(i, k, g_hbm, g_all, gs_sem, g_sem))
    for c in shares:
        c.start()

    load_reads.wait()
    load_counts.wait()

    picks = []
    for o in range(-SPAN, SPAN + 1):
        reader = along_seq(o)
        first = reads_ref[0, reader] - s * per_owner
        second = reads_ref[1, reader] - s * per_owner
        one = (first >= 0) & (first < per_owner)
        two = (second >= 0) & (second < per_owner)
        picks.append(jnp.where(one, first, jnp.where(two, second, 0)))

    def kv_copy(put, got, o, kind):
        g = o + SPAN
        return pltpu.make_async_remote_copy(
            src_ref=put.at[g],
            dst_ref=got.at[g],
            send_sem=kv_send.at[kind, g],
            recv_sem=kv_recv.at[kind, g],
            device_id=(along_seq(o), x),
            device_id_type=MESH,
        )

    load_k.wait()
    for o in offsets:
        put_k[o + SPAN] = own_k[picks[o + SPAN]]
        kv_copy(put_k, got_k, o, 0).start()
    got_k[SPAN] = own_k[picks[SPAN]]
    load_v.wait()
    for o in offsets:
        put_v[o + SPAN] = own_v[picks[o + SPAN]]
        kv_copy(put_v, got_v, o, 1).start()
    got_v[SPAN] = own_v[picks[SPAN]]

    def await_share(u):
        for buf, ssem, rsem in ((q_all, qs_sem, q_sem), (g_all, gs_sem, g_sem)):
            pltpu.make_async_remote_copy(
                src_ref=buf.at[u],
                dst_ref=buf.at[u],
                send_sem=ssem.at[u],
                recv_sem=rsem.at[u],
                device_id=(s, along_head(1)),
                device_id_type=MESH,
            ).wait_recv()

    images = [reads_ref[j, s] for j in range(READS)]
    groups = [
        jnp.minimum(lax.rem(s - (images[j] // per_owner) + SPAN + n_seq, n_seq), WIDTH - 1)
        for j in range(READS)
    ]
    limits = [counts_ref[images[j]] for j in range(READS)]
    sum_k[...] = jnp.zeros_like(sum_k)
    sum_v[...] = jnp.zeros_like(sum_v)
    for u in range(per_head):
        for c in own_load(u):
            c.wait()
    for o in offsets:
        kv_copy(put_k, got_k, o, 0).wait()
    for j in range(READS):
        keys[j * slots : (j + 1) * slots, :] = got_k[groups[j]]
    keys_t[...] = keys[...].T
    for o in offsets:
        kv_copy(put_v, got_v, o, 1).wait()
    for j in range(READS):
        values[j * slots : (j + 1) * slots, :] = got_v[groups[j]]

    def usable(i):
        return (i % tiles) < limits[i // tiles]

    half_slots = slots // 2
    chunk = 512
    n_chunks = READS * slots // chunk
    chunk_tiles = chunk // TILE
    halves = ((s0, d0), (s1, d1))

    def score_chunk(q, g, half, c):
        s_ref, d_ref = half
        rows = pl.ds(c * chunk, chunk)
        score = dot(keys[rows, :], q, NT)
        s_ref[rows, :] = score
        d_ref[rows, :] = dot(values[rows, :], g, NT)
        return [
            jnp.max(score[t * TILE : (t + 1) * TILE].reshape(TILE // 8, 8, UNIT), axis=0)
            for t in range(chunk_tiles)
        ]

    def finish_max(tops):
        top = None
        for i in range(n_tiles):
            one = jnp.where(usable(i), tops[i], -jnp.inf)
            top = one if top is None else jnp.maximum(top, one)
        return jnp.max(top, axis=0, keepdims=True) * SCALE2

    def first_scores():
        q, g = heads_to_rows(q_all[0]), heads_to_rows(g_all[0])
        tops = []
        for c in range(n_chunks):
            tops += score_chunk(q, g, halves[0], c)
        row_max[0:1, :] = finish_max(tops)

    def step(u, b, more):
        s_ref, d_ref = halves[b]
        top = row_max[b : b + 1, :]
        total = jnp.zeros((8, UNIT), F32)
        weighted = jnp.zeros((8, UNIT), F32)
        tops = []
        if more:
            qn, gn = heads_to_rows(q_all[u + 1]), heads_to_rows(g_all[u + 1])
        for c in range(n_chunks):
            if more:
                tops += score_chunk(qn, gn, halves[1 - b], c)
            for t in range(chunk_tiles):
                i = c * chunk_tiles + t
                rows = pl.ds(i * TILE, TILE)
                shift = jnp.where(usable(i), top, jnp.inf)
                p = jnp.exp2(s_ref[rows, :] * SCALE2 - shift)
                s_ref[rows, :] = p
                total = total + jnp.sum(p.reshape(TILE // 8, 8, UNIT), axis=0)
                weighted = weighted + jnp.sum(
                    (p * d_ref[rows, :]).reshape(TILE // 8, 8, UNIT), axis=0
                )
        if more:
            row_max[1 - b : 2 - b, :] = finish_max(tops)
        inverse = 1.0 / jnp.sum(total, axis=0, keepdims=True)
        row_dot = jnp.sum(weighted, axis=0, keepdims=True) * inverse
        q, g = heads_to_rows(q_all[u]), heads_to_rows(g_all[u])
        cols = pl.ds(pl.multiple_of(u * UNIT, UNIT), UNIT)
        q_rows[cols, :] = q
        g_rows[cols, :] = g
        dq = None
        for late in (False, True):
            for j in range(READS):
                start = j * slots + (half_slots if late else 0)
                for t in range(half_slots // TILE):
                    rows = pl.ds(start + t * TILE, TILE)
                    a = s_ref[rows, :] * inverse
                    low = a.astype(BF16)
                    grad = (a * (d_ref[rows, :] - row_dot)).astype(BF16)
                    if late:
                        kept = pl.ds(j * half_slots + t * TILE, TILE)
                        att_late[kept, cols] = low
                        dsc_late[kept, cols] = grad
                    else:
                        att[rows, :] = low
                        dsc[rows, :] = grad
                rows = pl.ds(start, half_slots)
                if late:
                    grad = dsc_late[pl.ds(j * half_slots, half_slots), cols]
                else:
                    grad = dsc[rows, :]
                    sum_v[rows, :] += dot(att[rows, :], g, NN)
                    sum_k[rows, :] += dot(grad, q, NN)
                part = dot(keys_t[:, start : start + half_slots], grad, NN)
                dq = part if dq is None else dq + part
        dq = (dq * SCALE).T.astype(BF16)
        for h in range(PAIRS):
            dq_all[u, :, h * HDIM : (h + 1) * HDIM] = dq[h * HDIM : (h + 1) * HDIM]

    def dq_own(u):
        cols = pl.ds(pl.multiple_of(x * head_cols + u * UNIT, UNIT), UNIT)
        return pltpu.make_async_copy(dq_all.at[u], dq_hbm.at[:, cols], dq_send.at[u])

    def dq_copy(u):
        r = u - per_head
        i = lax.div(r, n_head - 1)
        h = lax.rem(r, n_head - 1)
        hop = jnp.where(h == 0, HOPS[0], jnp.where(h == 1, HOPS[1], HOPS[2]))
        cols = pl.ds(pl.multiple_of(x * head_cols + i * UNIT, UNIT), UNIT)
        return pltpu.make_async_remote_copy(
            src_ref=dq_all.at[u],
            dst_ref=dq_hbm.at[:, cols],
            send_sem=dq_send.at[u],
            recv_sem=dq_recv.at[u],
            device_id=(s, lax.rem(x - hop + n_head, n_head)),
            device_id_type=MESH,
        )

    first_scores()
    for u in range(per_head - 1):
        step(u, u % 2, True)
        dq_own(u).start()
    await_share(per_head)
    step(per_head - 1, (per_head - 1) % 2, True)
    dq_own(per_head - 1).start()

    def two(j, carry):
        u = per_head + 2 * j
        await_share(u + 1)
        step(u, 0, True)
        dq_copy(u).start()
        await_share(u + 2)
        step(u + 1, 1, True)
        dq_copy(u + 1).start()
        return carry

    lax.fori_loop(0, (units - per_head) // 2 - 1, two, 0)
    await_share(units - 1)
    step(units - 2, 0, True)
    dq_copy(units - 2).start()
    step(units - 1, 1, False)
    dq_copy(units - 1).start()

    def back_copy(put, got, o, kind, half):
        g = o + SPAN
        rows = pl.ds(half * half_slots, half_slots)
        return pltpu.make_async_remote_copy(
            src_ref=put.at[g, rows],
            dst_ref=got.at[g, rows],
            send_sem=back_send.at[kind, half, g],
            recv_sem=back_recv.at[kind, half, g],
            device_id=(along_seq(-o), x),
            device_id_type=MESH,
        )

    which = []
    for g in range(WIDTH):
        which.append(jnp.where(groups[0] == g, 0, jnp.where(groups[1] == g, 1, READS)))

    def give_back(half):
        for low, total, factor, put, got, kind, late, rows_of in (
            (low_v, sum_v, None, put_v, ret_v, 1, att_late, g_rows),
            (low_k, sum_k, SCALE, put_k, ret_k, 0, dsc_late, q_rows),
        ):
            for j in range(READS):
                if half:
                    block = dot(late[j * half_slots : (j + 1) * half_slots, :], rows_of[...], NN)
                else:
                    block = total[j * slots : j * slots + half_slots, :]
                low[half, j] = (block if factor is None else block * factor).astype(BF16)
            low[half, READS] = jnp.zeros(low.shape[2:], BF16)
            rows = pl.ds(half * half_slots, half_slots)
            for o in offsets:
                put[o + SPAN, rows] = low[half, which[o + SPAN]]
                back_copy(put, got, o, kind, half).start()
            got[SPAN, rows] = low[half, which[SPAN]]

    def take_back(half):
        rows = pl.ds(half * half_slots, half_slots)
        for put, got, kind, out in ((put_v, ret_v, 1, out_v), (put_k, ret_k, 0, out_k)):
            for o in offsets:
                back_copy(put, got, o, kind, half).wait()
            for i in range(per_owner):
                acc = jnp.zeros((half_slots, HDIM), F32)
                for g in range(WIDTH):
                    acc = acc + jnp.where(picks[g] == i, got[g, rows].astype(F32), 0.0)
                out[i, rows] = acc.astype(BF16)

    give_back(0)
    give_back(1)
    take_back(0)
    take_back(1)

    for c in shares:
        c.wait_send()
    for u in range(per_head):
        dq_own(u).wait()

    def finish(j, carry):
        dq_copy(per_head + j).wait()
        return carry

    lax.fori_loop(0, units - per_head, finish, 0)


def write_out(*refs):
    sem = refs[-1]
    half = (len(refs) - 1) // 2
    copies = [
        pltpu.make_async_copy(refs[i], refs[half + i], sem.at[i]) for i in range(half)
    ]
    for c in copies:
        c.start()
    for c in copies:
        c.wait()


def per_device(queries, image_keys, image_values, out_grad, tile_counts, block_reads):
    n_seq, n_head = lax.axis_size("seq"), lax.axis_size("head")
    rows, cols = queries.shape
    per_owner, slots, _ = image_keys.shape
    head_cols = cols // n_head
    units = cols // UNIT
    sizes = (n_seq, n_head, per_owner, slots, head_cols)
    inside = pl.BlockSpec(memory_space=pltpu.VMEM)
    anywhere = pl.BlockSpec(memory_space=pl.ANY)
    image = (slots, HDIM)
    span = READS * slots
    vmem = pltpu.VMEM
    dma = pltpu.SemaphoreType.DMA
    operands = (tile_counts, block_reads.T, queries, image_keys, image_values, out_grad)
    grads = pl.pallas_call(
        functools.partial(kernel, sizes),
        out_shape=(
            pltpu.VMEM(queries.shape, BF16),
            pltpu.VMEM(image_keys.shape, BF16),
            pltpu.VMEM(image_values.shape, BF16),
        ),
        in_specs=[anywhere, anywhere, anywhere, anywhere, anywhere, anywhere],
        out_specs=[inside] * 3,
        scratch_shapes=[
            pltpu.SMEM(tile_counts.shape, jnp.int32),
            pltpu.SMEM(block_reads.shape[::-1], jnp.int32),
            vmem((per_owner, *image), BF16),
            vmem((per_owner, *image), BF16),
            vmem((WIDTH, *image), BF16),
            vmem((WIDTH, *image), BF16),
            vmem((WIDTH, *image), BF16),
            vmem((WIDTH, *image), BF16),
            vmem((WIDTH, *image), BF16),
            vmem((WIDTH, *image), BF16),
            vmem((units, rows, UNIT), BF16),
            vmem((units, rows, UNIT), BF16),
            vmem((units, rows, UNIT), BF16),
            vmem((span, HDIM), BF16),
            vmem((HDIM, span), BF16),
            vmem((span, HDIM), BF16),
            vmem((span, UNIT), F32),
            vmem((span, UNIT), F32),
            vmem((span, UNIT), F32),
            vmem((span, UNIT), F32),
            vmem((span, UNIT), BF16),
            vmem((span, UNIT), BF16),
            vmem((span // 2, units * UNIT), BF16),
            vmem((span // 2, units * UNIT), BF16),
            vmem((units * UNIT, HDIM), BF16),
            vmem((units * UNIT, HDIM), BF16),
            vmem((8, UNIT), F32),
            vmem((span, HDIM), F32),
            vmem((span, HDIM), F32),
            vmem((2, READS + 1, slots // 2, HDIM), BF16),
            vmem((2, READS + 1, slots // 2, HDIM), BF16),
            dma((4,)),
            dma((units,)),
            dma((units,)),
            dma((units,)),
            dma((units,)),
            dma((2, WIDTH)),
            dma((2, WIDTH)),
            dma((2, 2, WIDTH)),
            dma((2, 2, WIDTH)),
            dma((units,)),
            dma((units,)),
        ],
        compiler_params=pltpu.CompilerParams(
            collective_id=0, has_side_effects=True, vmem_limit_bytes=VMEM_LIMIT
        ),
        name="cross_attention_backward",
    )(*(pltpu.with_memory_space_constraint(a, pltpu.HBM) for a in operands))
    return pl.pallas_call(
        write_out,
        out_shape=[jax.ShapeDtypeStruct(a.shape, a.dtype) for a in grads],
        in_specs=[inside] * 3,
        out_specs=[anywhere] * 3,
        scratch_shapes=[dma((3,))],
        name="write_out",
    )(*(pltpu.with_memory_space_constraint(a, pltpu.VMEM) for a in grads))


def solution(mesh):
    in_specs = (
        P(("seq", "head"), None),
        P("seq", None, "head"),
        P("seq", None, "head"),
        P(("seq", "head"), None),
        P(),
        P(),
    )
    out_specs = (P(("seq", "head"), None), P("seq", None, "head"), P("seq", None, "head"))
    return jax.shard_map(
        per_device, mesh=mesh, in_specs=in_specs, out_specs=out_specs, check_vma=False
    )
```

```python
import functools

import jax
import jax.numpy as jnp
from jax import lax
from jax.experimental import pallas as pl
from jax.experimental.pallas import tpu as pltpu
from jax.sharding import PartitionSpec as P

HDIM = 128
TILE = 128
READS = 2
SPAN = 2
WIDTH = 2 * SPAN + 1
SCALE = HDIM ** (-0.5)
SCALE2 = SCALE * 1.4426950408889634
UNIT = 256
PAIRS = UNIT // HDIM
VMEM_LIMIT = 58 * 1024 * 1024
F32 = jnp.float32
BF16 = jnp.bfloat16
MESH = pl.DeviceIdType.MESH
NN = (((1,), (0,)), ((), ()))
NT = (((1,), (1,)), ((), ()))
HOPS = (1, 3, 2)


def dot(a, b, dims):
    return lax.dot_general(a, b, dims, preferred_element_type=F32)


def heads_to_rows(x):
    return jnp.concatenate([x[:, h * HDIM : (h + 1) * HDIM] for h in range(PAIRS)], axis=0)


def kernel(
    sizes,
    counts_hbm,
    reads_hbm,
    q_hbm,
    k_hbm,
    v_hbm,
    g_hbm,
    dq_hbm,
    out_k,
    out_v,
    counts_ref,
    reads_ref,
    own_k,
    own_v,
    put_k,
    put_v,
    got_k,
    got_v,
    ret_k,
    ret_v,
    q_all,
    g_all,
    dq_all,
    keys,
    keys_t,
    values,
    s0,
    d0,
    s1,
    d1,
    att,
    dsc,
    att_late,
    dsc_late,
    q_rows,
    g_rows,
    row_max,
    sum_k,
    sum_v,
    low_k,
    low_v,
    own_sem,
    q_sem,
    g_sem,
    qs_sem,
    gs_sem,
    kv_send,
    kv_recv,
    back_send,
    back_recv,
    dq_send,
    dq_recv,
):
    n_seq, n_head, per_owner, slots, head_cols = sizes
    per_head = head_cols // UNIT
    units = n_head * per_head
    n_tiles = READS * slots // TILE
    tiles = slots // TILE
    s = lax.axis_index("seq")
    x = lax.axis_index("head")

    def along_head(k):
        return lax.rem(x + k, n_head)

    def along_seq(o):
        return lax.rem(s + o + n_seq, n_seq)

    barrier = pltpu.get_barrier_semaphore()
    offsets = [o for o in range(-SPAN, SPAN + 1) if o != 0]
    for k in range(1, n_head):
        pl.semaphore_signal(barrier, inc=1, device_id=(s, along_head(k)), device_id_type=MESH)
    for o in offsets:
        pl.semaphore_signal(barrier, inc=1, device_id=(along_seq(o), x), device_id_type=MESH)

    load_reads = pltpu.make_async_copy(reads_hbm, reads_ref, own_sem.at[2])
    load_counts = pltpu.make_async_copy(counts_hbm, counts_ref, own_sem.at[3])
    load_reads.start()
    load_counts.start()
    load_k = pltpu.make_async_copy(k_hbm, own_k, own_sem.at[0])
    load_v = pltpu.make_async_copy(v_hbm, own_v, own_sem.at[1])
    load_k.start()
    load_v.start()

    def own_load(u):
        cols = pl.ds(pl.multiple_of(x * head_cols + u * UNIT, UNIT), UNIT)
        return (
            pltpu.make_async_copy(q_hbm.at[:, cols], q_all.at[u], q_sem.at[u]),
            pltpu.make_async_copy(g_hbm.at[:, cols], g_all.at[u], g_sem.at[u]),
        )

    for u in range(per_head):
        for c in own_load(u):
            c.start()

    pl.semaphore_wait(barrier, n_head - 1 + len(offsets))

    def share_copy(i, k, src, dst, ssem, rsem):
        u = per_head + (n_head - 1) * i + HOPS.index(k)
        to = along_head(k)
        cols = pl.ds(pl.multiple_of(to * head_cols + i * UNIT, UNIT), UNIT)
        return pltpu.make_async_remote_copy(
            src_ref=src.at[:, cols],
            dst_ref=dst.at[u],
            send_sem=ssem.at[u],
            recv_sem=rsem.at[u],
            device_id=(s, to),
            device_id_type=MESH,
        )

    shares = []
    for i in range(per_head):
        for k in HOPS:
            shares.append(share_copy(i, k, q_hbm, q_all, qs_sem, q_sem))
            shares.append(share_copy(i, k, g_hbm, g_all, gs_sem, g_sem))
    for c in shares:
        c.start()

    load_reads.wait()
    load_counts.wait()

    picks = []
    for o in range(-SPAN, SPAN + 1):
        reader = along_seq(o)
        first = reads_ref[0, reader] - s * per_owner
        second = reads_ref[1, reader] - s * per_owner
        one = (first >= 0) & (first < per_owner)
        two = (second >= 0) & (second < per_owner)
        picks.append(jnp.where(one, first, jnp.where(two, second, 0)))

    def kv_copy(put, got, o, kind):
        g = o + SPAN
        return pltpu.make_async_remote_copy(
            src_ref=put.at[g],
            dst_ref=got.at[g],
            send_sem=kv_send.at[kind, g],
            recv_sem=kv_recv.at[kind, g],
            device_id=(along_seq(o), x),
            device_id_type=MESH,
        )

    load_k.wait()
    for o in offsets:
        put_k[o + SPAN] = own_k[picks[o + SPAN]]
        kv_copy(put_k, got_k, o, 0).start()
    got_k[SPAN] = own_k[picks[SPAN]]
    load_v.wait()
    for o in offsets:
        put_v[o + SPAN] = own_v[picks[o + SPAN]]
        kv_copy(put_v, got_v, o, 1).start()
    got_v[SPAN] = own_v[picks[SPAN]]

    def await_share(u):
        for buf, ssem, rsem in ((q_all, qs_sem, q_sem), (g_all, gs_sem, g_sem)):
            pltpu.make_async_remote_copy(
                src_ref=buf.at[u],
                dst_ref=buf.at[u],
                send_sem=ssem.at[u],
                recv_sem=rsem.at[u],
                device_id=(s, along_head(1)),
                device_id_type=MESH,
            ).wait_recv()

    images = [reads_ref[j, s] for j in range(READS)]
    groups = [
        jnp.minimum(lax.rem(s - (images[j] // per_owner) + SPAN + n_seq, n_seq), WIDTH - 1)
        for j in range(READS)
    ]
    limits = [counts_ref[images[j]] for j in range(READS)]
    sum_k[...] = jnp.zeros_like(sum_k)
    sum_v[...] = jnp.zeros_like(sum_v)
    for u in range(per_head):
        for c in own_load(u):
            c.wait()
    for o in offsets:
        kv_copy(put_k, got_k, o, 0).wait()
    for j in range(READS):
        keys[j * slots : (j + 1) * slots, :] = got_k[groups[j]]
    keys_t[...] = keys[...].T
    for o in offsets:
        kv_copy(put_v, got_v, o, 1).wait()
    for j in range(READS):
        values[j * slots : (j + 1) * slots, :] = got_v[groups[j]]

    def usable(i):
        return (i % tiles) < limits[i // tiles]

    half_slots = slots // 2
    chunk = 512
    n_chunks = READS * slots // chunk
    chunk_tiles = chunk // TILE
    halves = ((s0, d0), (s1, d1))

    def score_chunk(q, g, half, c):
        s_ref, d_ref = half
        rows = pl.ds(c * chunk, chunk)
        score = dot(keys[rows, :], q, NT)
        s_ref[rows, :] = score
        d_ref[rows, :] = dot(values[rows, :], g, NT)
        return [
            jnp.max(score[t * TILE : (t + 1) * TILE].reshape(TILE // 8, 8, UNIT), axis=0)
            for t in range(chunk_tiles)
        ]

    def finish_max(tops):
        top = None
        for i in range(n_tiles):
            one = jnp.where(usable(i), tops[i], -jnp.inf)
            top = one if top is None else jnp.maximum(top, one)
        return jnp.max(top, axis=0, keepdims=True) * SCALE2

    def first_scores():
        q, g = heads_to_rows(q_all[0]), heads_to_rows(g_all[0])
        tops = []
        for c in range(n_chunks):
            tops += score_chunk(q, g, halves[0], c)
        row_max[0:1, :] = finish_max(tops)

    def step(u, b, more, values_done=None):
        s_ref, d_ref = halves[b]
        top = row_max[b : b + 1, :]
        total = jnp.zeros((8, UNIT), F32)
        weighted = jnp.zeros((8, UNIT), F32)
        tops = []
        if more:
            qn, gn = heads_to_rows(q_all[u + 1]), heads_to_rows(g_all[u + 1])
        for c in range(n_chunks):
            if more:
                tops += score_chunk(qn, gn, halves[1 - b], c)
            for t in range(chunk_tiles):
                i = c * chunk_tiles + t
                rows = pl.ds(i * TILE, TILE)
                shift = jnp.where(usable(i), top, jnp.inf)
                p = jnp.exp2(s_ref[rows, :] * SCALE2 - shift)
                s_ref[rows, :] = p
                total = total + jnp.sum(p.reshape(TILE // 8, 8, UNIT), axis=0)
                weighted = weighted + jnp.sum(
                    (p * d_ref[rows, :]).reshape(TILE // 8, 8, UNIT), axis=0
                )
        if more:
            row_max[1 - b : 2 - b, :] = finish_max(tops)
        inverse = 1.0 / jnp.sum(total, axis=0, keepdims=True)
        row_dot = jnp.sum(weighted, axis=0, keepdims=True) * inverse
        q, g = heads_to_rows(q_all[u]), heads_to_rows(g_all[u])
        cols = pl.ds(pl.multiple_of(u * UNIT, UNIT), UNIT)
        q_rows[cols, :] = q
        g_rows[cols, :] = g
        if values_done is not None:
            for j in range(READS):
                rows = pl.ds(j * slots, half_slots)
                for t in range(half_slots // TILE):
                    tile = pl.ds(j * slots + t * TILE, TILE)
                    att[tile, :] = (s_ref[tile, :] * inverse).astype(BF16)
                sum_v[rows, :] += dot(att[rows, :], g, NN)
            values_done()
        dq = None
        for late in (False, True):
            for j in range(READS):
                start = j * slots + (half_slots if late else 0)
                for t in range(half_slots // TILE):
                    rows = pl.ds(start + t * TILE, TILE)
                    a = s_ref[rows, :] * inverse
                    low = a.astype(BF16)
                    grad = (a * (d_ref[rows, :] - row_dot)).astype(BF16)
                    if late:
                        kept = pl.ds(j * half_slots + t * TILE, TILE)
                        att_late[kept, cols] = low
                        dsc_late[kept, cols] = grad
                    else:
                        if values_done is None:
                            att[rows, :] = low
                        dsc[rows, :] = grad
                rows = pl.ds(start, half_slots)
                if late:
                    grad = dsc_late[pl.ds(j * half_slots, half_slots), cols]
                else:
                    grad = dsc[rows, :]
                    if values_done is None:
                        sum_v[rows, :] += dot(att[rows, :], g, NN)
                    sum_k[rows, :] += dot(grad, q, NN)
                part = dot(keys_t[:, start : start + half_slots], grad, NN)
                dq = part if dq is None else dq + part
        dq = (dq * SCALE).T.astype(BF16)
        for h in range(PAIRS):
            dq_all[u, :, h * HDIM : (h + 1) * HDIM] = dq[h * HDIM : (h + 1) * HDIM]

    def dq_own(u):
        cols = pl.ds(pl.multiple_of(x * head_cols + u * UNIT, UNIT), UNIT)
        return pltpu.make_async_copy(dq_all.at[u], dq_hbm.at[:, cols], dq_send.at[u])

    def dq_copy(u):
        r = u - per_head
        i = lax.div(r, n_head - 1)
        h = lax.rem(r, n_head - 1)
        hop = jnp.where(h == 0, HOPS[0], jnp.where(h == 1, HOPS[1], HOPS[2]))
        cols = pl.ds(pl.multiple_of(x * head_cols + i * UNIT, UNIT), UNIT)
        return pltpu.make_async_remote_copy(
            src_ref=dq_all.at[u],
            dst_ref=dq_hbm.at[:, cols],
            send_sem=dq_send.at[u],
            recv_sem=dq_recv.at[u],
            device_id=(s, lax.rem(x - hop + n_head, n_head)),
            device_id_type=MESH,
        )

    def await_unit(u):
        @pl.when(u >= per_head)
        def _():
            await_share(u)

    def send_dq(u):
        @pl.when(u < per_head)
        def _():
            dq_own(u).start()

        @pl.when(u >= per_head)
        def _():
            dq_copy(u).start()

    def two(j, carry):
        u = 2 * j
        await_unit(u + 1)
        step(u, 0, True)
        send_dq(u)
        await_unit(u + 2)
        step(u + 1, 1, True)
        send_dq(u + 1)
        return carry

    def back_copy(put, got, o, kind, half):
        g = o + SPAN
        rows = pl.ds(half * half_slots, half_slots)
        return pltpu.make_async_remote_copy(
            src_ref=put.at[g, rows],
            dst_ref=got.at[g, rows],
            send_sem=back_send.at[kind, half, g],
            recv_sem=back_recv.at[kind, half, g],
            device_id=(along_seq(-o), x),
            device_id_type=MESH,
        )

    which = []
    for g in range(WIDTH):
        which.append(jnp.where(groups[0] == g, 0, jnp.where(groups[1] == g, 1, READS)))

    def give_back(half, kind):
        low, total, factor, put, got, late, rows_of = (
            (low_k, sum_k, SCALE, put_k, ret_k, dsc_late, q_rows),
            (low_v, sum_v, None, put_v, ret_v, att_late, g_rows),
        )[kind]
        for j in range(READS):
            if half:
                block = dot(late[j * half_slots : (j + 1) * half_slots, :], rows_of[...], NN)
            else:
                block = total[j * slots : j * slots + half_slots, :]
            low[half, j] = (block if factor is None else block * factor).astype(BF16)
        low[half, READS] = jnp.zeros(low.shape[2:], BF16)
        rows = pl.ds(half * half_slots, half_slots)
        for o in offsets:
            put[o + SPAN, rows] = low[half, which[o + SPAN]]
            back_copy(put, got, o, kind, half).start()
        got[SPAN, rows] = low[half, which[SPAN]]

    def take_back(half):
        rows = pl.ds(half * half_slots, half_slots)
        for put, got, kind, out in ((put_v, ret_v, 1, out_v), (put_k, ret_k, 0, out_k)):
            for o in offsets:
                back_copy(put, got, o, kind, half).wait()
            for i in range(per_owner):
                acc = jnp.zeros((half_slots, HDIM), F32)
                for g in range(WIDTH):
                    acc = acc + jnp.where(picks[g] == i, got[g, rows].astype(F32), 0.0)
                out[i, rows] = acc.astype(BF16)

    first_scores()
    lax.fori_loop(0, units // 2 - 1, two, 0)
    await_share(units - 1)
    step(units - 2, 0, True)
    dq_copy(units - 2).start()
    step(units - 1, 1, False, lambda: give_back(0, 1))
    dq_copy(units - 1).start()
    give_back(0, 0)
    give_back(1, 1)
    give_back(1, 0)
    for c in shares:
        c.wait_send()
    for u in range(per_head):
        dq_own(u).wait()
    take_back(0)

    def finish(j, carry):
        dq_copy(per_head + j).wait()
        return carry

    lax.fori_loop(0, units - per_head, finish, 0)
    take_back(1)


def write_out(*refs):
    sem = refs[-1]
    half = (len(refs) - 1) // 2
    copies = []
    for i in range(half):
        rows = refs[i].shape[0] // 4
        for r in range(4):
            part = pl.ds(r * rows, rows)
            copies.append(
                pltpu.make_async_copy(refs[i].at[part], refs[half + i].at[part], sem.at[i, r])
            )
    for c in copies:
        c.start()
    for c in copies:
        c.wait()


def per_device(queries, image_keys, image_values, out_grad, tile_counts, block_reads):
    n_seq, n_head = lax.axis_size("seq"), lax.axis_size("head")
    rows, cols = queries.shape
    per_owner, slots, _ = image_keys.shape
    head_cols = cols // n_head
    units = cols // UNIT
    sizes = (n_seq, n_head, per_owner, slots, head_cols)
    inside = pl.BlockSpec(memory_space=pltpu.VMEM)
    anywhere = pl.BlockSpec(memory_space=pl.ANY)
    image = (slots, HDIM)
    span = READS * slots
    vmem = pltpu.VMEM
    dma = pltpu.SemaphoreType.DMA
    operands = (tile_counts, block_reads.T, queries, image_keys, image_values, out_grad)
    grads = pl.pallas_call(
        functools.partial(kernel, sizes),
        out_shape=(
            pltpu.VMEM(queries.shape, BF16),
            pltpu.VMEM(image_keys.shape, BF16),
            pltpu.VMEM(image_values.shape, BF16),
        ),
        in_specs=[anywhere, anywhere, anywhere, anywhere, anywhere, anywhere],
        out_specs=[inside] * 3,
        scratch_shapes=[
            pltpu.SMEM(tile_counts.shape, jnp.int32),
            pltpu.SMEM(block_reads.shape[::-1], jnp.int32),
            vmem((per_owner, *image), BF16),
            vmem((per_owner, *image), BF16),
            vmem((WIDTH, *image), BF16),
            vmem((WIDTH, *image), BF16),
            vmem((WIDTH, *image), BF16),
            vmem((WIDTH, *image), BF16),
            vmem((WIDTH, *image), BF16),
            vmem((WIDTH, *image), BF16),
            vmem((units, rows, UNIT), BF16),
            vmem((units, rows, UNIT), BF16),
            vmem((units, rows, UNIT), BF16),
            vmem((span, HDIM), BF16),
            vmem((HDIM, span), BF16),
            vmem((span, HDIM), BF16),
            vmem((span, UNIT), F32),
            vmem((span, UNIT), F32),
            vmem((span, UNIT), F32),
            vmem((span, UNIT), F32),
            vmem((span, UNIT), BF16),
            vmem((span, UNIT), BF16),
            vmem((span // 2, units * UNIT), BF16),
            vmem((span // 2, units * UNIT), BF16),
            vmem((units * UNIT, HDIM), BF16),
            vmem((units * UNIT, HDIM), BF16),
            vmem((8, UNIT), F32),
            vmem((span, HDIM), F32),
            vmem((span, HDIM), F32),
            vmem((2, READS + 1, slots // 2, HDIM), BF16),
            vmem((2, READS + 1, slots // 2, HDIM), BF16),
            dma((4,)),
            dma((units,)),
            dma((units,)),
            dma((units,)),
            dma((units,)),
            dma((2, WIDTH)),
            dma((2, WIDTH)),
            dma((2, 2, WIDTH)),
            dma((2, 2, WIDTH)),
            dma((units,)),
            dma((units,)),
        ],
        compiler_params=pltpu.CompilerParams(
            collective_id=0, has_side_effects=True, vmem_limit_bytes=VMEM_LIMIT
        ),
        name="cross_attention_backward",
    )(*(pltpu.with_memory_space_constraint(a, pltpu.HBM) for a in operands))
    return pl.pallas_call(
        write_out,
        out_shape=[jax.ShapeDtypeStruct(a.shape, a.dtype) for a in grads],
        in_specs=[inside] * 3,
        out_specs=[anywhere] * 3,
        scratch_shapes=[dma((3, 4))],
        name="write_out",
    )(*(pltpu.with_memory_space_constraint(a, pltpu.VMEM) for a in grads))


def solution(mesh):
    in_specs = (
        P(("seq", "head"), None),
        P("seq", None, "head"),
        P("seq", None, "head"),
        P(("seq", "head"), None),
        P(),
        P(),
    )
    out_specs = (P(("seq", "head"), None), P("seq", None, "head"), P("seq", None, "head"))
    return jax.shard_map(
        per_device, mesh=mesh, in_specs=in_specs, out_specs=out_specs, check_vma=False
    )
```

```python
import functools

import jax
import jax.numpy as jnp
from jax import lax
from jax.experimental import pallas as pl
from jax.experimental.pallas import tpu as pltpu
from jax.sharding import PartitionSpec as P

HDIM = 128
TILE = 128
READS = 2
SPAN = 2
WIDTH = 2 * SPAN + 1
SCALE = HDIM ** (-0.5)
SCALE2 = SCALE * 1.4426950408889634
UNIT = 256
PAIRS = UNIT // HDIM
VMEM_LIMIT = 58 * 1024 * 1024
F32 = jnp.float32
BF16 = jnp.bfloat16
MESH = pl.DeviceIdType.MESH
NN = (((1,), (0,)), ((), ()))
NT = (((1,), (1,)), ((), ()))
HOPS = (1, 3, 2)


def dot(a, b, dims):
    return lax.dot_general(a, b, dims, preferred_element_type=F32)


def heads_to_rows(x):
    return jnp.concatenate([x[:, h * HDIM : (h + 1) * HDIM] for h in range(PAIRS)], axis=0)


def kernel(
    sizes,
    counts_hbm,
    reads_hbm,
    q_hbm,
    k_hbm,
    v_hbm,
    g_hbm,
    dq_hbm,
    out_k,
    out_v,
    counts_ref,
    reads_ref,
    own_k,
    own_v,
    put_k,
    put_v,
    got_k,
    got_v,
    ret_k,
    ret_v,
    q_all,
    g_all,
    dq_all,
    keys,
    keys_t,
    values,
    s0,
    d0,
    s1,
    d1,
    att,
    dsc,
    att_late,
    dsc_late,
    q_rows,
    g_rows,
    row_max,
    sum_k,
    sum_v,
    low_k,
    low_v,
    own_sem,
    q_sem,
    g_sem,
    qs_sem,
    gs_sem,
    kv_send,
    kv_recv,
    back_send,
    back_recv,
    dq_send,
    dq_recv,
):
    n_seq, n_head, per_owner, slots, head_cols = sizes
    per_head = head_cols // UNIT
    units = n_head * per_head
    n_tiles = READS * slots // TILE
    tiles = slots // TILE
    s = lax.axis_index("seq")
    x = lax.axis_index("head")

    def along_head(k):
        return lax.rem(x + k, n_head)

    def along_seq(o):
        return lax.rem(s + o + n_seq, n_seq)

    barrier = pltpu.get_barrier_semaphore()
    offsets = [o for d in range(SPAN, 0, -1) for o in (-d, d)]
    for k in range(1, n_head):
        pl.semaphore_signal(barrier, inc=1, device_id=(s, along_head(k)), device_id_type=MESH)
    for o in offsets:
        pl.semaphore_signal(barrier, inc=1, device_id=(along_seq(o), x), device_id_type=MESH)

    load_reads = pltpu.make_async_copy(reads_hbm, reads_ref, own_sem.at[2])
    load_counts = pltpu.make_async_copy(counts_hbm, counts_ref, own_sem.at[3])
    load_reads.start()
    load_counts.start()
    load_k = pltpu.make_async_copy(k_hbm, own_k, own_sem.at[0])
    load_v = pltpu.make_async_copy(v_hbm, own_v, own_sem.at[1])
    load_k.start()
    load_v.start()

    def own_load(u):
        cols = pl.ds(pl.multiple_of(x * head_cols + u * UNIT, UNIT), UNIT)
        return (
            pltpu.make_async_copy(q_hbm.at[:, cols], q_all.at[u], q_sem.at[u]),
            pltpu.make_async_copy(g_hbm.at[:, cols], g_all.at[u], g_sem.at[u]),
        )

    for u in range(per_head):
        for c in own_load(u):
            c.start()

    pl.semaphore_wait(barrier, n_head - 1 + len(offsets))

    def share_copy(i, k, src, dst, ssem, rsem):
        u = per_head + (n_head - 1) * i + HOPS.index(k)
        to = along_head(k)
        cols = pl.ds(pl.multiple_of(to * head_cols + i * UNIT, UNIT), UNIT)
        return pltpu.make_async_remote_copy(
            src_ref=src.at[:, cols],
            dst_ref=dst.at[u],
            send_sem=ssem.at[u],
            recv_sem=rsem.at[u],
            device_id=(s, to),
            device_id_type=MESH,
        )

    shares = []
    for i in range(per_head):
        for k in HOPS:
            shares.append(share_copy(i, k, q_hbm, q_all, qs_sem, q_sem))
            shares.append(share_copy(i, k, g_hbm, g_all, gs_sem, g_sem))
    for c in shares:
        c.start()

    load_reads.wait()
    load_counts.wait()

    picks = []
    for o in range(-SPAN, SPAN + 1):
        reader = along_seq(o)
        first = reads_ref[0, reader] - s * per_owner
        second = reads_ref[1, reader] - s * per_owner
        one = (first >= 0) & (first < per_owner)
        two = (second >= 0) & (second < per_owner)
        picks.append(jnp.where(one, first, jnp.where(two, second, 0)))

    def kv_copy(put, got, o, kind):
        g = o + SPAN
        return pltpu.make_async_remote_copy(
            src_ref=put.at[g],
            dst_ref=got.at[g],
            send_sem=kv_send.at[kind, g],
            recv_sem=kv_recv.at[kind, g],
            device_id=(along_seq(o), x),
            device_id_type=MESH,
        )

    load_k.wait()
    for o in offsets:
        put_k[o + SPAN] = own_k[picks[o + SPAN]]
        kv_copy(put_k, got_k, o, 0).start()
    got_k[SPAN] = own_k[picks[SPAN]]
    load_v.wait()
    for o in offsets:
        put_v[o + SPAN] = own_v[picks[o + SPAN]]
        kv_copy(put_v, got_v, o, 1).start()
    got_v[SPAN] = own_v[picks[SPAN]]

    def await_share(u):
        for buf, ssem, rsem in ((q_all, qs_sem, q_sem), (g_all, gs_sem, g_sem)):
            pltpu.make_async_remote_copy(
                src_ref=buf.at[u],
                dst_ref=buf.at[u],
                send_sem=ssem.at[u],
                recv_sem=rsem.at[u],
                device_id=(s, along_head(1)),
                device_id_type=MESH,
            ).wait_recv()

    images = [reads_ref[j, s] for j in range(READS)]
    groups = [
        jnp.minimum(lax.rem(s - (images[j] // per_owner) + SPAN + n_seq, n_seq), WIDTH - 1)
        for j in range(READS)
    ]
    limits = [counts_ref[images[j]] for j in range(READS)]
    sum_k[...] = jnp.zeros_like(sum_k)
    sum_v[...] = jnp.zeros_like(sum_v)
    for u in range(per_head):
        for c in own_load(u):
            c.wait()
    for o in offsets:
        kv_copy(put_k, got_k, o, 0).wait()
    for j in range(READS):
        keys[j * slots : (j + 1) * slots, :] = got_k[groups[j]]
    keys_t[...] = keys[...].T
    for o in offsets:
        kv_copy(put_v, got_v, o, 1).wait()
    for j in range(READS):
        values[j * slots : (j + 1) * slots, :] = got_v[groups[j]]

    def usable(i):
        return (i % tiles) < limits[i // tiles]

    half_slots = slots // 2
    chunk = 1024
    n_chunks = READS * slots // chunk
    chunk_tiles = chunk // TILE
    halves = ((s0, d0), (s1, d1))

    def score_chunk(q, g, half, c):
        s_ref, d_ref = half
        rows = pl.ds(c * chunk, chunk)
        score = dot(keys[rows, :], q, NT)
        s_ref[rows, :] = score
        d_ref[rows, :] = dot(values[rows, :], g, NT)
        return [
            jnp.max(score[t * TILE : (t + 1) * TILE].reshape(TILE // 8, 8, UNIT), axis=0)
            for t in range(chunk_tiles)
        ]

    def finish_max(tops):
        top = None
        for i in range(n_tiles):
            one = jnp.where(usable(i), tops[i], -jnp.inf)
            top = one if top is None else jnp.maximum(top, one)
        return jnp.max(top, axis=0, keepdims=True) * SCALE2

    def first_scores():
        q, g = heads_to_rows(q_all[0]), heads_to_rows(g_all[0])
        tops = []
        for c in range(n_chunks):
            tops += score_chunk(q, g, halves[0], c)
        row_max[0:1, :] = finish_max(tops)

    def step(u, b, more, values_done=None):
        s_ref, d_ref = halves[b]
        top = row_max[b : b + 1, :]
        total = jnp.zeros((8, UNIT), F32)
        weighted = jnp.zeros((8, UNIT), F32)
        tops = []
        if more:
            qn, gn = heads_to_rows(q_all[u + 1]), heads_to_rows(g_all[u + 1])
        for c in range(n_chunks):
            if more:
                tops += score_chunk(qn, gn, halves[1 - b], c)
            for t in range(chunk_tiles):
                i = c * chunk_tiles + t
                rows = pl.ds(i * TILE, TILE)
                shift = jnp.where(usable(i), top, jnp.inf)
                p = jnp.exp2(s_ref[rows, :] * SCALE2 - shift)
                s_ref[rows, :] = p
                total = total + jnp.sum(p.reshape(TILE // 8, 8, UNIT), axis=0)
                weighted = weighted + jnp.sum(
                    (p * d_ref[rows, :]).reshape(TILE // 8, 8, UNIT), axis=0
                )
        if more:
            row_max[1 - b : 2 - b, :] = finish_max(tops)
        inverse = 1.0 / jnp.sum(total, axis=0, keepdims=True)
        row_dot = jnp.sum(weighted, axis=0, keepdims=True) * inverse
        q, g = heads_to_rows(q_all[u]), heads_to_rows(g_all[u])
        cols = pl.ds(pl.multiple_of(u * UNIT, UNIT), UNIT)
        q_rows[cols, :] = q
        g_rows[cols, :] = g
        if values_done is not None:
            for j in range(READS):
                rows = pl.ds(j * slots, half_slots)
                for t in range(half_slots // TILE):
                    tile = pl.ds(j * slots + t * TILE, TILE)
                    att[tile, :] = (s_ref[tile, :] * inverse).astype(BF16)
                sum_v[rows, :] += dot(att[rows, :], g, NN)
            values_done()
        dq = None
        for late in (False, True):
            for j in range(READS):
                start = j * slots + (half_slots if late else 0)
                for t in range(half_slots // TILE):
                    rows = pl.ds(start + t * TILE, TILE)
                    a = s_ref[rows, :] * inverse
                    low = a.astype(BF16)
                    grad = (a * (d_ref[rows, :] - row_dot)).astype(BF16)
                    if late:
                        kept = pl.ds(j * half_slots + t * TILE, TILE)
                        att_late[kept, cols] = low
                        dsc_late[kept, cols] = grad
                    else:
                        if values_done is None:
                            att[rows, :] = low
                        dsc[rows, :] = grad
                rows = pl.ds(start, half_slots)
                if late:
                    grad = dsc_late[pl.ds(j * half_slots, half_slots), cols]
                else:
                    grad = dsc[rows, :]
                    if values_done is None:
                        sum_v[rows, :] += dot(att[rows, :], g, NN)
                    sum_k[rows, :] += dot(grad, q, NN)
                part = dot(keys_t[:, start : start + half_slots], grad, NN)
                dq = part if dq is None else dq + part
        dq = (dq * SCALE).T.astype(BF16)
        for h in range(PAIRS):
            dq_all[u, :, h * HDIM : (h + 1) * HDIM] = dq[h * HDIM : (h + 1) * HDIM]

    def dq_own(u):
        cols = pl.ds(pl.multiple_of(x * head_cols + u * UNIT, UNIT), UNIT)
        return pltpu.make_async_copy(dq_all.at[u], dq_hbm.at[:, cols], dq_send.at[u])

    def dq_copy(u):
        r = u - per_head
        i = lax.div(r, n_head - 1)
        h = lax.rem(r, n_head - 1)
        hop = jnp.where(h == 0, HOPS[0], jnp.where(h == 1, HOPS[1], HOPS[2]))
        cols = pl.ds(pl.multiple_of(x * head_cols + i * UNIT, UNIT), UNIT)
        return pltpu.make_async_remote_copy(
            src_ref=dq_all.at[u],
            dst_ref=dq_hbm.at[:, cols],
            send_sem=dq_send.at[u],
            recv_sem=dq_recv.at[u],
            device_id=(s, lax.rem(x - hop + n_head, n_head)),
            device_id_type=MESH,
        )

    def await_unit(u):
        @pl.when(u >= per_head)
        def _():
            await_share(u)

    def send_dq(u):
        @pl.when(u < per_head)
        def _():
            dq_own(u).start()

        @pl.when(u >= per_head)
        def _():
            dq_copy(u).start()

    def two(j, carry):
        u = 2 * j
        await_unit(u + 1)
        step(u, 0, True)
        send_dq(u)
        await_unit(u + 2)
        step(u + 1, 1, True)
        send_dq(u + 1)
        return carry

    def back_copy(put, got, o, kind, half):
        g = o + SPAN
        rows = pl.ds(half * half_slots, half_slots)
        return pltpu.make_async_remote_copy(
            src_ref=put.at[g, rows],
            dst_ref=got.at[g, rows],
            send_sem=back_send.at[kind, half, g],
            recv_sem=back_recv.at[kind, half, g],
            device_id=(along_seq(-o), x),
            device_id_type=MESH,
        )

    which = []
    for g in range(WIDTH):
        which.append(jnp.where(groups[0] == g, 0, jnp.where(groups[1] == g, 1, READS)))

    def give_back(half, kind):
        low, total, factor, put, got, late, rows_of = (
            (low_k, sum_k, SCALE, put_k, ret_k, dsc_late, q_rows),
            (low_v, sum_v, None, put_v, ret_v, att_late, g_rows),
        )[kind]
        for j in range(READS):
            if half:
                block = dot(late[j * half_slots : (j + 1) * half_slots, :], rows_of[...], NN)
            else:
                block = total[j * slots : j * slots + half_slots, :]
            low[half, j] = (block if factor is None else block * factor).astype(BF16)
        low[half, READS] = jnp.zeros(low.shape[2:], BF16)
        rows = pl.ds(half * half_slots, half_slots)
        for o in offsets:
            put[o + SPAN, rows] = low[half, which[o + SPAN]]
            back_copy(put, got, o, kind, half).start()
        got[SPAN, rows] = low[half, which[SPAN]]

    def take_back(half):
        rows = pl.ds(half * half_slots, half_slots)
        for put, got, kind, out in ((put_v, ret_v, 1, out_v), (put_k, ret_k, 0, out_k)):
            for o in offsets:
                back_copy(put, got, o, kind, half).wait()
            for i in range(per_owner):
                acc = jnp.zeros((half_slots, HDIM), F32)
                for g in range(WIDTH):
                    acc = acc + jnp.where(picks[g] == i, got[g, rows].astype(F32), 0.0)
                out[i, rows] = acc.astype(BF16)

    first_scores()
    lax.fori_loop(0, units // 2 - 1, two, 0)
    await_share(units - 1)
    step(units - 2, 0, True)
    dq_copy(units - 2).start()
    step(units - 1, 1, False, lambda: give_back(0, 1))
    dq_copy(units - 1).start()
    give_back(0, 0)
    give_back(1, 1)
    give_back(1, 0)
    for c in shares:
        c.wait_send()
    for u in range(per_head):
        dq_own(u).wait()
    take_back(0)

    def finish(j, carry):
        dq_copy(per_head + j).wait()
        return carry

    lax.fori_loop(0, units - per_head, finish, 0)
    take_back(1)


def write_out(*refs):
    sem = refs[-1]
    half = (len(refs) - 1) // 2
    copies = []
    for i in range(half):
        rows = refs[i].shape[0] // 4
        for r in range(4):
            part = pl.ds(r * rows, rows)
            copies.append(
                pltpu.make_async_copy(refs[i].at[part], refs[half + i].at[part], sem.at[i, r])
            )
    for c in copies:
        c.start()
    for c in copies:
        c.wait()


def per_device(queries, image_keys, image_values, out_grad, tile_counts, block_reads):
    n_seq, n_head = lax.axis_size("seq"), lax.axis_size("head")
    rows, cols = queries.shape
    per_owner, slots, _ = image_keys.shape
    head_cols = cols // n_head
    units = cols // UNIT
    sizes = (n_seq, n_head, per_owner, slots, head_cols)
    inside = pl.BlockSpec(memory_space=pltpu.VMEM)
    anywhere = pl.BlockSpec(memory_space=pl.ANY)
    image = (slots, HDIM)
    span = READS * slots
    vmem = pltpu.VMEM
    dma = pltpu.SemaphoreType.DMA
    operands = (tile_counts, block_reads.T, queries, image_keys, image_values, out_grad)
    grads = pl.pallas_call(
        functools.partial(kernel, sizes),
        out_shape=(
            pltpu.VMEM(queries.shape, BF16),
            pltpu.VMEM(image_keys.shape, BF16),
            pltpu.VMEM(image_values.shape, BF16),
        ),
        in_specs=[anywhere, anywhere, anywhere, anywhere, anywhere, anywhere],
        out_specs=[inside] * 3,
        scratch_shapes=[
            pltpu.SMEM(tile_counts.shape, jnp.int32),
            pltpu.SMEM(block_reads.shape[::-1], jnp.int32),
            vmem((per_owner, *image), BF16),
            vmem((per_owner, *image), BF16),
            vmem((WIDTH, *image), BF16),
            vmem((WIDTH, *image), BF16),
            vmem((WIDTH, *image), BF16),
            vmem((WIDTH, *image), BF16),
            vmem((WIDTH, *image), BF16),
            vmem((WIDTH, *image), BF16),
            vmem((units, rows, UNIT), BF16),
            vmem((units, rows, UNIT), BF16),
            vmem((units, rows, UNIT), BF16),
            vmem((span, HDIM), BF16),
            vmem((HDIM, span), BF16),
            vmem((span, HDIM), BF16),
            vmem((span, UNIT), F32),
            vmem((span, UNIT), F32),
            vmem((span, UNIT), F32),
            vmem((span, UNIT), F32),
            vmem((span, UNIT), BF16),
            vmem((span, UNIT), BF16),
            vmem((span // 2, units * UNIT), BF16),
            vmem((span // 2, units * UNIT), BF16),
            vmem((units * UNIT, HDIM), BF16),
            vmem((units * UNIT, HDIM), BF16),
            vmem((8, UNIT), F32),
            vmem((span, HDIM), F32),
            vmem((span, HDIM), F32),
            vmem((2, READS + 1, slots // 2, HDIM), BF16),
            vmem((2, READS + 1, slots // 2, HDIM), BF16),
            dma((4,)),
            dma((units,)),
            dma((units,)),
            dma((units,)),
            dma((units,)),
            dma((2, WIDTH)),
            dma((2, WIDTH)),
            dma((2, 2, WIDTH)),
            dma((2, 2, WIDTH)),
            dma((units,)),
            dma((units,)),
        ],
        compiler_params=pltpu.CompilerParams(
            collective_id=0, has_side_effects=True, vmem_limit_bytes=VMEM_LIMIT
        ),
        name="cross_attention_backward",
    )(*(pltpu.with_memory_space_constraint(a, pltpu.HBM) for a in operands))
    return pl.pallas_call(
        write_out,
        out_shape=[jax.ShapeDtypeStruct(a.shape, a.dtype) for a in grads],
        in_specs=[inside] * 3,
        out_specs=[anywhere] * 3,
        scratch_shapes=[dma((3, 4))],
        name="write_out",
    )(*(pltpu.with_memory_space_constraint(a, pltpu.VMEM) for a in grads))


def solution(mesh):
    in_specs = (
        P(("seq", "head"), None),
        P("seq", None, "head"),
        P("seq", None, "head"),
        P(("seq", "head"), None),
        P(),
        P(),
    )
    out_specs = (P(("seq", "head"), None), P("seq", None, "head"), P("seq", None, "head"))
    return jax.shard_map(
        per_device, mesh=mesh, in_specs=in_specs, out_specs=out_specs, check_vma=False
    )
```
